256 devices in a mesh: kb: 16 (over z, core), pb: 16 (over y, x).
Axes of the slice: x: 4, y: 4, z: 8, core: 2. Of those that a mesh axis runs over, the one named last changes fastest.
Arguments:
- screened: bfloat16 [16, 2, 2048, 2048], P('pb', None, 'kb'), may hold values from -0.09375 to 0.09375
- elem_val: bfloat16 [96, 16, 2, 64, 2048], P('kb', 'pb'), may hold values from -6 to 6
- elem_cond: bfloat16 [96, 16, 2, 64, 2048], P('kb', 'pb'), may hold values from -0.09375 to 0.09375
- pair_first: int32 [96, 16], P('kb', 'pb'), may hold values from 0 to 63, as said below
- pair_second: int32 [96, 16], P('kb', 'pb'), may hold values from 0 to 63, as said below
- coeffs: float32 [64, 2], P('kb'), may hold values from -6 to 6
Outputs:
- kernel_applied: float32 [64, 2, 4096], P('kb', None, 'pb')
The draws below stay inside these ranges and needn't reach their ends.
Inputs may be any that keep to these rules, and one draw needn't show every extreme that they name: `pair_first`: slot rows s with s // 6 = b hold first k points in b * 4 to (b + 1) * 4 - 1. Each pair lies in the Hermitian half: pair_second is at least pair_first.
All inputs are finite; a program needn't handle non-finite values.
Results may differ from the reference program's by a relative error of at most 0.0029.
Values may be sent and summed in bfloat16 or wider, within the bound.
A program may use at most 192 MiB of HBM per device.

```python
import jax
import jax.numpy as jnp
from jax import lax

NG = 2048
NV = 64
NC = 64
PSLOT = 6
KDEV = 4
Q = 16
NK = 64
SLOTS = 96


def first_points(key):
    key = jax.random.fold_in(key, 11)
    blocks = jnp.arange(SLOTS, dtype=jnp.int32) // PSLOT * KDEV
    offsets = jax.random.randint(key, (SLOTS, Q), 0, KDEV, dtype=jnp.int32)
    return blocks[:, None] + offsets


def draw_pair_first(key, part):
    return first_points(key)


def draw_pair_second(key, part):
    firsts = first_points(key)
    key = jax.random.fold_in(key, 23)
    raw = jax.random.randint(key, (SLOTS, Q), 0, NK, dtype=jnp.int32)
    return firsts + raw % (NK - firsts)


def shard_levels(rng, dims, shards, low, high):
    def one(position, parts):
        heights = jax.random.uniform(jax.random.fold_in(jax.random.fold_in(rng, 6), position), (parts,), jnp.float32, low / len(shards), high / len(shards))
        return jnp.repeat(jnp.exp(heights), dims[position] // parts).reshape((-1,) + (1,) * (len(dims) - position - 1))

    level = one(*shards[0])
    for cut in shards[1:]:
        level = level * one(*cut)
    return level


def gaussian(own_key, shape, deviation, bound, pieces=(), held_as=jnp.bfloat16):
    result = jax.random.normal(own_key, shape, jnp.float32) * deviation
    if len(pieces) > 0:
        result = shard_levels(own_key, shape, pieces, -0.22, 0.18) * result
    return jnp.clip(result, min=-bound, max=bound).astype(held_as)


def setup_inputs(seed: int = 0) -> dict:
    splits = jax.random.split(jax.random.key(seed), 7)
    return {
        "screened": gaussian(splits[0], (Q, 2, NG, NG), (2 * NG) ** -0.5, 0.09375, ((0, 16), (2, 16))),
        "elem_val": gaussian(splits[1], (SLOTS, Q, 2, NV, NG), 1.0, 6.0, ((0, 16), (1, 16))),
        "elem_cond": gaussian(splits[2], (SLOTS, Q, 2, NC, NG), (2 * NG) ** -0.5, 0.09375, ((0, 16), (1, 16))),
        "pair_first": draw_pair_first(jax.random.fold_in(splits[6], 71), 0),
        "pair_second": draw_pair_second(jax.random.fold_in(splits[6], 71), 0),
        "coeffs": gaussian(splits[5], (NK, 2), 1.0, 6.0, ((0, 16),), jnp.float32),
    }


def screened_apply(weights, values):
    wgt = weights.astype(jnp.float32)
    val = values.astype(jnp.float32)
    real_part = jnp.einsum("gh,pvh->pgv", wgt[0], val[:, 0]) - jnp.einsum("gh,pvh->pgv", wgt[1], val[:, 1])
    imag_part = jnp.einsum("gh,pvh->pgv", wgt[0], val[:, 1]) + jnp.einsum("gh,pvh->pgv", wgt[1], val[:, 0])
    return real_part.astype(jnp.bfloat16), imag_part.astype(jnp.bfloat16)


def kernel_blocks(conds, real_part, imag_part):
    cond_re = conds[:, 0].astype(jnp.float32)
    cond_im = conds[:, 1].astype(jnp.float32)
    image_re = real_part.astype(jnp.float32)
    image_im = imag_part.astype(jnp.float32)
    block_re = jnp.einsum("pcg,pgv->pcv", cond_re, image_re) + jnp.einsum("pcg,pgv->pcv", cond_im, image_im)
    block_im = jnp.einsum("pcg,pgv->pcv", cond_re, image_im) - jnp.einsum("pcg,pgv->pcv", cond_im, image_re)
    return jnp.stack((block_re, block_im), axis=1)


def reference(screened, elem_val, elem_cond, pair_first, pair_second, coeffs):
    def one_transfer(inputs):
        weights, values, conds = inputs
        real_part, imag_part = screened_apply(weights, values)
        return kernel_blocks(conds, real_part, imag_part)

    blocks = lax.map(one_transfer, (screened, jnp.swapaxes(elem_val, 0, 1), jnp.swapaxes(elem_cond, 0, 1)))
    blocks = jnp.swapaxes(blocks, 0, 1)
    chosen = coeffs[pair_second.astype(jnp.int32)]
    coef_re = chosen[:, :, 0][:, :, None, None]
    coef_im = chosen[:, :, 1][:, :, None, None]
    term_re = blocks[:, :, 0] * coef_re - blocks[:, :, 1] * coef_im
    term_im = blocks[:, :, 0] * coef_im + blocks[:, :, 1] * coef_re
    terms = jnp.stack((term_re, term_im), axis=2).reshape(SLOTS * Q, 2, NC * NV)
    return jax.ops.segment_sum(terms, pair_first.reshape(-1).astype(jnp.int32), num_segments=NK)
```

```python
import functools

import jax
import jax.numpy as jnp
from jax import lax
from jax.experimental import pallas as pl
from jax.experimental.pallas import tpu as pltpu
from jax.sharding import PartitionSpec as P

MESH = pl.DeviceIdType.MESH
CHUNKS = 4
UP, DOWN = 0, 1


def kernel(
    ring, transfers, w_hbm, val_hbm, cond_hbm, first_ref, second_ref, coef_ref, out_ref,
    w_all, val, val_t, cond, image, acc, table, picked, stage, landed,
    local_sem, ring_send, ring_recv, pair_send, pair_recv, own_send, own_recv,
    coef_send, coef_recv, coef_pair_send, coef_pair_recv, sum_send, sum_recv,
):
    half = ring // 2
    rows = w_hbm.shape[2]
    chunk = rows // CHUNKS
    slots = cond.shape[0]
    local_k = coef_ref.shape[1]
    bands = cond.shape[1] // 2
    kb, pb = lax.axis_index("kb"), lax.axis_index("pb")
    z, core = kb // 2, kb % 2
    sibling = kb + 1 - 2 * core
    up = lax.rem(z + 1, ring) * 2 + core
    down = lax.rem(z + ring - 1, ring) * 2 + core

    def level(direction, hop):
        return lax.rem(z + ring - hop, ring) if direction == UP else lax.rem(z + hop, ring)

    def piece(block, index):
        return w_all.at[block, :, pl.ds(pl.multiple_of(index * chunk, chunk), chunk), :]

    def ring_out(direction, hop, index):
        block = 2 * level(direction, hop - 1) + core
        if isinstance(hop, int) and hop == 1:
            src = w_hbm.at[0, :, pl.ds(index * chunk, chunk), :]
        else:
            src = piece(block, index)
        place = (hop - 1) * CHUNKS + index
        return pltpu.make_async_remote_copy(
            src_ref=src, dst_ref=piece(block, index),
            send_sem=ring_send.at[direction, place], recv_sem=ring_recv.at[direction, place],
            device_id={"kb": up if direction == UP else down}, device_id_type=MESH,
        )

    def ring_in(direction, hop, index):
        block = 2 * level(direction, hop) + core
        place = (hop - 1) * CHUNKS + index
        return pltpu.make_async_remote_copy(
            src_ref=piece(block, index), dst_ref=piece(block, index),
            send_sem=ring_send.at[direction, place], recv_sem=ring_recv.at[direction, place],
            device_id={"kb": up if direction == UP else down}, device_id_type=MESH,
        )

    def pair(direction, hop, index, owner):
        block = 2 * level(direction, hop) + owner
        place = (hop - 1) * CHUNKS + index
        return pltpu.make_async_remote_copy(
            src_ref=piece(block, index), dst_ref=piece(block, index),
            send_sem=pair_send.at[direction, place], recv_sem=pair_recv.at[direction, place],
            device_id={"kb": sibling}, device_id_type=MESH,
        )

    def own_pair(owner):
        return pltpu.make_async_remote_copy(
            src_ref=w_hbm.at[0], dst_ref=w_all.at[owner], send_sem=own_send, recv_sem=own_recv,
            device_id={"kb": sibling}, device_id_type=MESH,
        )

    def coef_pair(owner):
        return pltpu.make_async_remote_copy(
            src_ref=table.at[owner], dst_ref=table.at[owner], send_sem=coef_pair_send, recv_sem=coef_pair_recv,
            device_id={"kb": sibling}, device_id_type=MESH,
        )

    def coef_ring(direction, hop, at):
        both = table.at[pl.ds(2 * at, 2)]
        return pltpu.make_async_remote_copy(
            src_ref=both, dst_ref=both,
            send_sem=coef_send.at[direction, hop - 1], recv_sem=coef_recv.at[direction, hop - 1],
            device_id={"kb": up if direction == UP else down}, device_id_type=MESH,
        )

    def partial_sum(distance):
        return pltpu.make_async_remote_copy(
            src_ref=stage.at[lax.rem(pb + distance, transfers)], dst_ref=landed.at[distance],
            send_sem=sum_send.at[distance], recv_sem=sum_recv.at[distance],
            device_id={"pb": lax.rem(pb + distance, transfers)}, device_id_type=MESH,
        )

    lane = lax.broadcasted_iota(jnp.int32, (1, 2 * bands), 1)
    minus_plus = jnp.where(lane < bands, -1.0, 1.0)

    def turn(block):
        return pltpu.roll(block, bands, axis=1) * minus_plus

    def make_image(pieces):
        rows_in = jnp.concatenate(
            [
                w_all[block, part, pl.ds(pl.multiple_of(index * chunk, chunk), chunk), :]
                for block, index, _, _ in pieces
                for part in range(2)
            ],
            axis=0,
        )
        for pair_of in range(slots // 2):
            wide = slice(pair_of * 4 * bands, (pair_of + 1) * 4 * bands)
            product = jnp.dot(rows_in, val_t[:, wide], preferred_element_type=jnp.float32)
            for i, (_, _, buffer, row) in enumerate(pieces):
                by_real = product[2 * i * chunk : (2 * i + 1) * chunk]
                by_imag = product[(2 * i + 1) * chunk : (2 * i + 2) * chunk]
                for s in range(2):
                    lanes = slice(s * 2 * bands, (s + 1) * 2 * bands)
                    to = (pair_of * 2 + s) * 2 * bands
                    image[buffer, pl.ds(pl.multiple_of(row, chunk), chunk), to : to + 2 * bands] = (
                        by_real[:, lanes] + turn(by_imag[:, lanes])
                    ).astype(jnp.bfloat16)

    def make_blocks(at, buffer):
        columns = pl.ds(pl.multiple_of(at * 2 * rows, 2 * rows), 2 * rows)
        for s in range(slots):
            acc[s] += jnp.dot(
                cond[s, :, columns],
                image[buffer, :, s * 2 * bands : (s + 1) * 2 * bands],
                preferred_element_type=jnp.float32,
            )

    loads = [
        pltpu.make_async_copy(val_hbm, val, local_sem.at[0]),
        pltpu.make_async_copy(w_hbm.at[0], w_all.at[kb], local_sem.at[1]),
        pltpu.make_async_copy(cond_hbm, cond, local_sem.at[2]),
    ]
    for load in loads:
        load.start()

    barrier = pltpu.get_barrier_semaphore()
    for other in (up, down, sibling):
        pl.semaphore_signal(barrier, inc=1, device_id={"kb": other}, device_id_type=MESH)
    for distance in range(1, transfers):
        pl.semaphore_signal(
            barrier, inc=1, device_id={"pb": lax.rem(pb + distance, transfers)}, device_id_type=MESH
        )
    pl.semaphore_wait(barrier, 3 + transfers - 1)

    for index in range(CHUNKS):
        ring_out(UP, 1, index).start()
        ring_out(DOWN, 1, CHUNKS - 1 - index).start()
    own_pair(kb).start()

    table[kb] = jnp.zeros_like(table[0])
    table[kb, 0:2, 0:local_k] = coef_ref[...]
    coef_pair(kb).start()
    acc[...] = jnp.zeros_like(acc)
    loads[0].wait()
    for k in range(val.shape[1] // 256):
        val_t[k * 256 : (k + 1) * 256, :] = val[:, k * 256 : (k + 1) * 256].T
    coef_pair(sibling).wait_recv()
    coef_ring(UP, 1, z).start()
    coef_ring(DOWN, 1, z).start()
    loads[1].wait()
    own_pair(sibling).wait_recv()

    def own_step(step, carry):
        make_image([
            (2 * z + owner, 2 * step + i, 0, owner * rows + (2 * step + i) * chunk)
            for i in range(2) for owner in range(2)
        ])
        return carry

    lax.fori_loop(0, CHUNKS // 2, own_step, 0)
    loads[2].wait()
    make_blocks(z, 0)

    def ring_step(step, carry):
        hop, index = step // CHUNKS + 1, step % CHUNKS
        ring_in(UP, hop, index).wait_recv()

        @pl.when((hop < half - 1) | (index < CHUNKS // 2))
        def _():
            ring_out(UP, hop + 1, index).start()

        pair(UP, hop, index, core).start()
        ring_in(DOWN, hop, CHUNKS - 1 - index).wait_recv()

        @pl.when((hop < half - 1) | (index < CHUNKS // 2))
        def _():
            ring_out(DOWN, hop + 1, CHUNKS - 1 - index).start()

        pair(DOWN, hop, CHUNKS - 1 - index, core).start()

        @pl.when(index == 0)
        def _():
            coef_ring(UP, hop, level(UP, hop)).wait_recv()
            coef_ring(UP, hop + 1, level(UP, hop)).start()
            coef_ring(DOWN, hop, level(DOWN, hop)).wait_recv()

            @pl.when(hop < half - 1)
            def _():
                coef_ring(DOWN, hop + 1, level(DOWN, hop)).start()

        pair(UP, hop, index, 1 - core).wait_recv()
        pair(DOWN, hop, CHUNKS - 1 - index, 1 - core).wait_recv()
        make_image([
            (2 * level(direction, hop) + owner, at, direction, owner * rows + at * chunk)
            for direction, at in ((UP, index), (DOWN, CHUNKS - 1 - index))
            for owner in range(2)
        ])

        @pl.when(index == CHUNKS - 1)
        def _():
            make_blocks(level(UP, hop), UP)
            make_blocks(level(DOWN, hop), DOWN)

        return carry

    lax.fori_loop(0, (half - 1) * CHUNKS, ring_step, 0)

    own_pair(kb).wait_send()
    coef_pair(kb).wait_send()

    def sent_step(step, carry):
        hop, index = step // CHUNKS + 1, step % CHUNKS
        for direction in (UP, DOWN):
            ring_in(direction, hop, index).wait_send()
            pair(direction, hop, index, core).wait_send()
        return carry

    lax.fori_loop(0, (half - 1) * CHUNKS, sent_step, 0)
    for hop in range(1, half):
        for direction in (UP, DOWN):
            coef_ring(direction, hop, z).wait_send()
    coef_ring(UP, half, z).wait_send()
    coef_ring(UP, half, level(UP, half)).wait_recv()

    where_block = lax.broadcasted_iota(jnp.int32, table.shape, 0)
    where_lane = lax.broadcasted_iota(jnp.int32, table.shape, 2)
    point = jnp.where(where_lane < local_k, where_block * local_k + where_lane, -1)
    coefs = table[...]
    for s in range(slots):
        chosen = jnp.sum(jnp.where(point == second_ref[0, s], coefs, 0.0), axis=0)
        chosen = jnp.sum(chosen, axis=1, keepdims=True)
        picked[2 * s : 2 * s + 2, :] = jnp.broadcast_to(chosen[0:2, :], (2, picked.shape[1]))

    def last_step(index, carry):
        ring_in(UP, half, index).wait_recv()
        pair(UP, half, index, core).start()
        ring_in(DOWN, half, CHUNKS - 1 - index).wait_recv()
        pair(DOWN, half, CHUNKS - 1 - index, core).start()
        pair(UP, half, index, 1 - core).wait_recv()
        pair(DOWN, half, CHUNKS - 1 - index, 1 - core).wait_recv()
        make_image([
            (2 * level(UP, half) + owner, at, 0, owner * rows + at * chunk)
            for at in (index, CHUNKS - 1 - index)
            for owner in range(2)
        ])
        return carry

    lax.fori_loop(0, CHUNKS // 2, last_step, 0)
    make_blocks(level(UP, half), 0)

    totals = [jnp.zeros((bands, 2 * bands), jnp.float32) for _ in range(local_k)]
    for s in range(slots):
        block = acc[s, 0:bands, :] - turn(acc[s, bands:, :])
        term = block * picked[2 * s : 2 * s + 1, :] + turn(block) * picked[2 * s + 1 : 2 * s + 2, :]
        owner = first_ref[0, s] - kb * local_k
        for k in range(local_k):
            totals[k] += jnp.where(owner == k, term, 0.0)
    take = bands // transfers
    for k in range(local_k):
        for to in range(transfers):
            stage[to, k * take : (k + 1) * take, :] = totals[k][to * take : (to + 1) * take, :]
    for distance in range(1, transfers):
        partial_sum(distance).start()
    for index in range(CHUNKS // 2):
        for direction, at in ((UP, index), (DOWN, CHUNKS - 1 - index)):
            ring_in(direction, half, at).wait_send()
            pair(direction, half, at, core).wait_send()
    total = stage[pb]
    for distance in range(1, transfers):
        partial_sum(distance).wait_recv()
        total += landed[distance]
    for k in range(local_k):
        for i in range(take // 2):
            even = total[k * take + 2 * i : k * take + 2 * i + 1, :]
            odd = total[k * take + 2 * i + 1 : k * take + 2 * i + 2, :]
            lanes = slice(i * 2 * bands, (i + 1) * 2 * bands)
            out_ref[k, 0:1, lanes] = jnp.where(lane < bands, even, pltpu.roll(odd, bands, axis=1))
            out_ref[k, 1:2, lanes] = jnp.where(lane < bands, pltpu.roll(even, bands, axis=1), odd)
    for distance in range(1, transfers):
        partial_sum(distance).wait_send()


def body(ring, transfers, screened, elem_val, elem_cond, pair_first, pair_second, coeffs):
    slots, _, _, bands, depth = elem_val.shape
    rows = screened.shape[2]
    local_k = coeffs.shape[0]
    half = ring // 2
    take = bands // transfers
    hbm = pl.BlockSpec(memory_space=pltpu.HBM)
    smem = pl.BlockSpec(memory_space=pltpu.SMEM)
    vmem = pl.BlockSpec(memory_space=pltpu.VMEM)
    dma = pltpu.SemaphoreType.DMA
    width = slots * 2 * bands
    return pl.pallas_call(
        functools.partial(kernel, ring, transfers),
        out_shape=jax.ShapeDtypeStruct((local_k, 2, take * bands), jnp.float32),
        in_specs=[hbm, hbm, hbm, smem, smem, vmem],
        out_specs=vmem,
        scratch_shapes=[
            pltpu.VMEM((2 * ring, 2, rows, depth), jnp.bfloat16),
            pltpu.VMEM((width, depth), jnp.bfloat16),
            pltpu.VMEM((depth, width), jnp.bfloat16),
            pltpu.VMEM((slots, 2 * bands, depth), jnp.bfloat16),
            pltpu.VMEM((2, 2 * rows, width), jnp.bfloat16),
            pltpu.VMEM((slots, 2 * bands, 2 * bands), jnp.float32),
            pltpu.VMEM((2 * ring, 8, 128), jnp.float32),
            pltpu.VMEM((2 * slots, 128), jnp.float32),
            pltpu.VMEM((transfers, local_k * take, 2 * bands), jnp.float32),
            pltpu.VMEM((transfers, local_k * take, 2 * bands), jnp.float32),
            dma((3,)),
            dma((2, half * CHUNKS)),
            dma((2, half * CHUNKS)),
            dma((2, half * CHUNKS)),
            dma((2, half * CHUNKS)),
            dma(()),
            dma(()),
            dma((2, half)),
            dma((2, half)),
            dma(()),
            dma(()),
            dma((transfers,)),
            dma((transfers,)),
        ],
        compiler_params=pltpu.CompilerParams(
            collective_id=0, has_side_effects=True, vmem_limit_bytes=56 * 1024 * 1024
        ),
        cost_estimate=pl.CostEstimate(
            flops=8 * depth * depth * slots * bands, bytes_accessed=8 * 1024 * 1024, transcendentals=0
        ),
    )(
        screened, elem_val.reshape(width, depth), elem_cond.reshape(slots, 2 * bands, depth),
        pair_first.T, pair_second.T, coeffs.T,
    )


def solution(mesh):
    in_specs = (
        P("pb", None, "kb", None),
        P("kb", "pb", None, None, None),
        P("kb", "pb", None, None, None),
        P("kb", "pb"),
        P("kb", "pb"),
        P("kb", None),
    )
    out_specs = P("kb", None, "pb")
    ring, transfers = mesh.shape["kb"] // 2, mesh.shape["pb"]
    return jax.shard_map(
        functools.partial(body, ring, transfers), mesh=mesh, in_specs=in_specs, out_specs=out_specs, check_vma=False
    )
```

```python
import functools

import jax
import jax.numpy as jnp
from jax import lax
from jax.experimental import pallas as pl
from jax.experimental.pallas import tpu as pltpu
from jax.sharding import PartitionSpec as P

MESH = pl.DeviceIdType.MESH
CHUNKS = 4
FLIGHT = 2
UP, DOWN = 0, 1


def side_of(transfers):
    return 1 << ((transfers.bit_length() - 1) // 2)


def rounds_of(transfers):
    side = side_of(transfers)
    return max(side // 2 + transfers // side // 2 - 1, 1)


def kernel(
    ring, transfers, w_hbm, val_hbm, cond_hbm, first_hbm, second_hbm, coef_hbm, out_ref,
    w_all, val, val_t, cond, image, acc, table, picked, stage, landed, first, second, coef,
    local_sem, ring_send, ring_recv, pair_send, pair_recv, own_recv,
    coef_send, coef_recv, coef_pair_recv, sum_send, sum_recv, known,
):
    half = ring // 2
    rows = w_hbm.shape[2]
    chunk = rows // CHUNKS
    slots = cond.shape[0]
    local_k = coef.shape[1]
    bands = cond.shape[1] // 2
    far_first = sorted(range(1, transfers), key=lambda distance: abs(distance - transfers // 2))
    total_sends = half * CHUNKS - CHUNKS // 2
    kb, pb = lax.axis_index("kb"), lax.axis_index("pb")
    z, core = kb // 2, kb % 2
    sibling = kb + 1 - 2 * core
    up = lax.rem(z + 1, ring) * 2 + core
    down = lax.rem(z + ring - 1, ring) * 2 + core

    side = side_of(transfers)
    y, x = pb // side, pb % side
    plane = [
        lax.rem(y + dy, transfers // side) * side + lax.rem(x + dx, side)
        for dy, dx in sorted({
            (1 % (transfers // side), 0), (transfers // side - 1, 0), (0, 1 % side), (0, side - 1)
        } - {(0, 0)})
    ]

    def level(direction, hop):
        return lax.rem(z + ring - hop, ring) if direction == UP else lax.rem(z + hop, ring)

    def place(direction, index):
        return index if direction == UP else CHUNKS - 1 - index

    def piece(block, index):
        return w_all.at[block, :, pl.ds(pl.multiple_of(index * chunk, chunk), chunk), :]

    def ring_copy(direction, number, src_hop):
        hop, index = number // CHUNKS + src_hop, place(direction, number % CHUNKS)
        block = 2 * level(direction, hop) + core
        return pltpu.make_async_remote_copy(
            src_ref=piece(block, index), dst_ref=piece(block, index),
            send_sem=ring_send, recv_sem=ring_recv.at[direction, number],
            device_id={"kb": up if direction == UP else down}, device_id_type=MESH,
        )

    def first_copy(direction, number):
        index = place(direction, number)
        return pltpu.make_async_remote_copy(
            src_ref=w_hbm.at[0, :, pl.ds(index * chunk, chunk), :], dst_ref=piece(kb, index),
            send_sem=ring_send, recv_sem=ring_recv.at[direction, number],
            device_id={"kb": up if direction == UP else down}, device_id_type=MESH,
        )

    def pair(direction, number, owner):
        hop, index = number // CHUNKS + 1, place(direction, number % CHUNKS)
        block = 2 * level(direction, hop) + owner
        return pltpu.make_async_remote_copy(
            src_ref=piece(block, index), dst_ref=piece(block, index),
            send_sem=pair_send, recv_sem=pair_recv.at[number],
            device_id={"kb": sibling}, device_id_type=MESH,
        )

    def remote(src, dst, send_sem, recv_sem, device):
        return pltpu.make_async_remote_copy(
            src_ref=src, dst_ref=dst, send_sem=send_sem, recv_sem=recv_sem, device_id=device, device_id_type=MESH
        )

    def arrived(ref, sem):
        pltpu.make_async_copy(ref, ref, sem).wait()

    def own_pair(owner):
        return remote(w_hbm.at[0], w_all.at[owner], pair_send, own_recv, {"kb": sibling})

    def coef_pair(owner):
        return remote(table.at[owner], table.at[owner], coef_send, coef_pair_recv, {"kb": sibling})

    def coef_ring(direction, hop, at):
        both = table.at[pl.ds(2 * at, 2)]
        return remote(
            both, both, coef_send, coef_recv.at[direction, hop - 1], {"kb": up if direction == UP else down}
        )

    lane = lax.broadcasted_iota(jnp.int32, (1, 2 * bands), 1)
    minus_plus = jnp.where(lane < bands, -1.0, 1.0)

    def turn(block):
        return pltpu.roll(block, bands, axis=1) * minus_plus

    def make_image(pieces):
        rows_in = jnp.concatenate(
            [
                w_all[block, part, pl.ds(pl.multiple_of(index * chunk, chunk), chunk), :]
                for block, index, _, _ in pieces
                for part in range(2)
            ],
            axis=0,
        )
        for pair_of in range(slots // 2):
            wide = slice(pair_of * 4 * bands, (pair_of + 1) * 4 * bands)
            product = jnp.dot(rows_in, val_t[:, wide], preferred_element_type=jnp.float32)
            for i, (_, _, buffer, row) in enumerate(pieces):
                by_real = product[2 * i * chunk : (2 * i + 1) * chunk]
                by_imag = product[(2 * i + 1) * chunk : (2 * i + 2) * chunk]
                for s in range(2):
                    lanes = slice(s * 2 * bands, (s + 1) * 2 * bands)
                    to = (pair_of * 2 + s) * 2 * bands
                    image[buffer, pl.ds(pl.multiple_of(row, chunk), chunk), to : to + 2 * bands] = (
                        by_real[:, lanes] + turn(by_imag[:, lanes])
                    ).astype(jnp.bfloat16)

    def make_blocks(at, buffer):
        columns = pl.ds(pl.multiple_of(at * 2 * rows, 2 * rows), 2 * rows)
        for s in range(slots):
            acc[s] += jnp.dot(
                cond[s, :, columns],
                image[buffer, :, s * 2 * bands : (s + 1) * 2 * bands],
                preferred_element_type=jnp.float32,
            )

    loads = [
        pltpu.make_async_copy(src, dst, local_sem.at[i])
        for i, (src, dst) in enumerate((
            (coef_hbm, coef), (val_hbm, val), (w_hbm.at[0], w_all.at[kb]), (cond_hbm, cond),
            (first_hbm, first), (second_hbm, second),
        ))
    ]
    barrier = pltpu.get_barrier_semaphore()
    for other in (up, down, sibling):
        pl.semaphore_signal(barrier, inc=1, device_id={"kb": other}, device_id_type=MESH)
    for other in plane:
        pl.semaphore_signal(barrier, inc=1, device_id={"pb": other}, device_id_type=MESH)
    pl.semaphore_wait(barrier, 3 + len(plane))

    for number in range(FLIGHT):
        first_copy(UP, number).start()
        first_copy(DOWN, number).start()
    own_pair(kb).start()
    for load in loads:
        load.start()

    table[kb] = jnp.zeros_like(table[0])
    loads[0].wait()
    table[kb, 0:2, 0:local_k] = coef[...]
    coef_pair(kb).start()
    acc[...] = jnp.zeros_like(acc)
    loads[1].wait()

    def transpose(k, carry):
        columns = pl.ds(pl.multiple_of(k * 256, 256), 256)
        val_t[columns, :] = val[:, columns].T
        return carry

    lax.fori_loop(0, val.shape[1] // 256, transpose, 0)
    coef_pair(sibling).wait_recv()
    coef_ring(UP, 1, z).start()
    coef_ring(DOWN, 1, z).start()
    for load in loads[2:]:
        load.wait()
    own_pair(sibling).wait_recv()

    def step(at, carry):
        hop, index = at // CHUNKS, at % CHUNKS
        number = at - CHUNKS

        @pl.when(hop > 0)
        def _():
            later = number + FLIGHT
            for direction in (UP, DOWN):
                ring_copy(direction, number, 1).wait_recv()
                pl.when(later < total_sends)(lambda direction=direction: ring_copy(direction, later, 0).start())
                pair(direction, number, core).start()

        @pl.when((hop > 0) & (index == 1) & (hop <= rounds_of(transfers)))
        def _():
            for other in plane:
                pl.semaphore_signal(known.at[hop - 1], inc=1, device_id={"pb": other}, device_id_type=MESH)

        @pl.when((hop > 0) & (index == CHUNKS - 1) & (hop <= rounds_of(transfers)))
        def _():
            pl.semaphore_wait(known.at[hop - 1], len(plane))

        @pl.when((hop > 0) & (index == 0))
        def _():
            coef_ring(UP, hop, level(UP, hop)).wait_recv()

            @pl.when(hop < half)
            def _():
                coef_ring(UP, hop + 1, level(UP, hop)).start()
                coef_ring(DOWN, hop, level(DOWN, hop)).wait_recv()

            @pl.when(hop < half - 1)
            def _():
                coef_ring(DOWN, hop + 1, level(DOWN, hop)).start()

            @pl.when(hop == half)
            def _():
                where_block = lax.broadcasted_iota(jnp.int32, table.shape, 0)
                where_lane = lax.broadcasted_iota(jnp.int32, table.shape, 2)
                point = jnp.where(where_lane < local_k, where_block * local_k + where_lane, -1)
                coefs = table[...]
                for s in range(slots):
                    chosen = jnp.sum(jnp.where(point == second[0, s], coefs, 0.0), axis=0)
                    chosen = jnp.sum(chosen, axis=1, keepdims=True)
                    picked[2 * s : 2 * s + 2, :] = jnp.broadcast_to(chosen[0:2, :], (2, picked.shape[1]))

        @pl.when(hop > 0)
        def _():
            arrived(w_all.at[pl.ds(0, 2), :, pl.ds(0, chunk), :], pair_recv.at[number])

        between = (hop > 0) & (hop < half)
        make_image([
            (2 * level(direction, hop) + owner, at_row, buffer, owner * rows + at_row * chunk)
            for direction, at_row, buffer in (
                (UP, place(UP, index), 0), (DOWN, place(DOWN, index), jnp.where(between, 1, 0)),
            )
            for owner in range(2)
        ])

        @pl.when(index == jnp.where(hop == half, CHUNKS // 2 - 1, CHUNKS - 1))
        def _():
            def blocks(buffer, carry):
                make_blocks(jnp.where(buffer == 0, level(UP, hop), level(DOWN, hop)), buffer)
                return carry

            lax.fori_loop(0, jnp.where(between, 2, 1), blocks, 0)

        return carry

    lax.fori_loop(CHUNKS // 2, half * CHUNKS + CHUNKS // 2, step, 0)

    totals = [jnp.zeros((bands, 2 * bands), jnp.float32) for _ in range(local_k)]
    for s in range(slots):
        block = acc[s, 0:bands, :] - turn(acc[s, bands:, :])
        term = block * picked[2 * s : 2 * s + 1, :] + turn(block) * picked[2 * s + 1 : 2 * s + 2, :]
        owner = first[0, s] - kb * local_k
        for k in range(local_k):
            totals[k] += jnp.where(owner == k, term, 0.0)
    take = bands // transfers
    for k in range(local_k):
        for to in range(transfers):
            stage[to, k * take : (k + 1) * take, :] = totals[k][to * take : (to + 1) * take, :]
    for i, distance in enumerate(far_first):
        to = lax.rem(pb + distance, transfers)
        remote(stage.at[to], landed.at[i], sum_send, sum_recv, {"pb": to}).start()
    arrived(w_all.at[pl.ds(0, ring - 1)], ring_send)
    arrived(w_all.at[pl.ds(0, ring)], pair_send)
    arrived(table.at[pl.ds(0, 1 + 2 * (2 * half - 1))], coef_send)
    total = stage[pb]
    arrived(landed.at[pl.ds(0, transfers - 1)], sum_recv)
    for i in range(transfers - 1):
        total += landed[i]
    for k in range(local_k):
        for i in range(take // 2):
            even = total[k * take + 2 * i : k * take + 2 * i + 1, :]
            odd = total[k * take + 2 * i + 1 : k * take + 2 * i + 2, :]
            lanes = slice(i * 2 * bands, (i + 1) * 2 * bands)
            out_ref[k, 0:1, lanes] = jnp.where(lane < bands, even, pltpu.roll(odd, bands, axis=1))
            out_ref[k, 1:2, lanes] = jnp.where(lane < bands, pltpu.roll(even, bands, axis=1), odd)
    arrived(landed.at[pl.ds(0, transfers - 1)], sum_send)


def body(ring, transfers, screened, elem_val, elem_cond, pair_first, pair_second, coeffs):
    slots, _, _, bands, depth = elem_val.shape
    rows = screened.shape[2]
    local_k = coeffs.shape[0]
    half = ring // 2
    take = bands // transfers
    dma = pltpu.SemaphoreType.DMA
    width = slots * 2 * bands
    return pl.pallas_call(
        functools.partial(kernel, ring, transfers),
        out_shape=jax.ShapeDtypeStruct((local_k, 2, take * bands), jnp.float32),
        in_specs=[pl.BlockSpec(memory_space=pltpu.HBM)] * 6,
        out_specs=pl.BlockSpec(memory_space=pltpu.VMEM),
        scratch_shapes=[
            pltpu.VMEM((2 * ring, 2, rows, depth), jnp.bfloat16),
            pltpu.VMEM((width, depth), jnp.bfloat16),
            pltpu.VMEM((depth, width), jnp.bfloat16),
            pltpu.VMEM((slots, 2 * bands, depth), jnp.bfloat16),
            pltpu.VMEM((2, 2 * rows, width), jnp.bfloat16),
            pltpu.VMEM((slots, 2 * bands, 2 * bands), jnp.float32),
            pltpu.VMEM((2 * ring, 8, 128), jnp.float32),
            pltpu.VMEM((2 * slots, 128), jnp.float32),
            pltpu.VMEM((transfers, local_k * take, 2 * bands), jnp.float32),
            pltpu.VMEM((transfers, local_k * take, 2 * bands), jnp.float32),
            pltpu.SMEM((1, slots), jnp.int32),
            pltpu.SMEM((1, slots), jnp.int32),
            pltpu.VMEM((2, local_k), jnp.float32),
            dma((6,)),
            dma(()),
            dma((2, half * CHUNKS - CHUNKS // 2)),
            dma(()),
            dma((half * CHUNKS - CHUNKS // 2,)),
            dma(()),
            dma(()),
            dma((2, half)),
            dma(()),
            dma(()),
            dma(()),
            pltpu.SemaphoreType.REGULAR((rounds_of(transfers),)),
        ],
        compiler_params=pltpu.CompilerParams(
            collective_id=0, has_side_effects=True, vmem_limit_bytes=40 * 1024 * 1024
        ),
        cost_estimate=pl.CostEstimate(
            flops=8 * depth * depth * slots * bands, bytes_accessed=8 * 1024 * 1024, transcendentals=0
        ),
    )(*(
        pltpu.with_memory_space_constraint(operand, pltpu.HBM)
        for operand in (
            screened, elem_val.reshape(width, depth), elem_cond.reshape(slots, 2 * bands, depth),
            pair_first.T, pair_second.T, coeffs.T,
        )
    ))


def solution(mesh):
    in_specs = (
        P("pb", None, "kb", None),
        P("kb", "pb", None, None, None),
        P("kb", "pb", None, None, None),
        P("kb", "pb"),
        P("kb", "pb"),
        P("kb", None),
    )
    out_specs = P("kb", None, "pb")
    ring, transfers = mesh.shape["kb"] // 2, mesh.shape["pb"]
    return jax.shard_map(
        functools.partial(body, ring, transfers), mesh=mesh, in_specs=in_specs, out_specs=out_specs, check_vma=False
    )
```

```python
import functools

import jax
import jax.numpy as jnp
from jax import lax
from jax.experimental import pallas as pl
from jax.experimental.pallas import tpu as pltpu
from jax.sharding import PartitionSpec as P

MESH = pl.DeviceIdType.MESH
CHUNKS = 4
FLIGHT = 2
TAIL = 4
UP, DOWN = 0, 1


def side_of(transfers):
    return 1 << ((transfers.bit_length() - 1) // 2)


def rounds_of(transfers):
    side = side_of(transfers)
    return max(side // 2 + transfers // side // 2 - 1, 1)


def kernel(
    ring, transfers, w_hbm, val_hbm, cond_hbm, first_hbm, second_hbm, coef_hbm, out_ref,
    w_all, val, val_t, cond, image, acc, table, picked, stage, landed, first, second, coef,
    local_sem, ring_send, ring_recv, pair_send, pair_recv, own_recv,
    coef_send, coef_recv, coef_pair_recv, sum_send, sum_recv, known,
):
    half = ring // 2
    rows = w_hbm.shape[2]
    chunk = rows // CHUNKS
    slots = cond.shape[0]
    local_k = coef.shape[1]
    bands = cond.shape[1] // 2
    far_first = sorted(range(1, transfers), key=lambda distance: abs(distance - transfers // 2))
    full = (half - 1) * CHUNKS
    short = rows // 2 // TAIL
    kb, pb = lax.axis_index("kb"), lax.axis_index("pb")
    z, core = kb // 2, kb % 2
    sibling = kb + 1 - 2 * core
    up = lax.rem(z + 1, ring) * 2 + core
    down = lax.rem(z + ring - 1, ring) * 2 + core

    side = side_of(transfers)
    y, x = pb // side, pb % side
    plane = [
        lax.rem(y + dy, transfers // side) * side + lax.rem(x + dx, side)
        for dy, dx in sorted({
            (1 % (transfers // side), 0), (transfers // side - 1, 0), (0, 1 % side), (0, side - 1)
        } - {(0, 0)})
    ]

    def level(direction, hop):
        return lax.rem(z + ring - hop, ring) if direction == UP else lax.rem(z + hop, ring)

    def place(direction, index):
        return index if direction == UP else CHUNKS - 1 - index

    def piece(block, index):
        return w_all.at[block, :, pl.ds(pl.multiple_of(index * chunk, chunk), chunk), :]

    def ring_copy(direction, number, src_hop):
        hop, index = number // CHUNKS + src_hop, place(direction, number % CHUNKS)
        block = 2 * level(direction, hop) + core
        return pltpu.make_async_remote_copy(
            src_ref=piece(block, index), dst_ref=piece(block, index),
            send_sem=ring_send, recv_sem=ring_recv.at[direction, number],
            device_id={"kb": up if direction == UP else down}, device_id_type=MESH,
        )

    def first_copy(direction, number):
        index = place(direction, number)
        return pltpu.make_async_remote_copy(
            src_ref=w_hbm.at[0, :, pl.ds(index * chunk, chunk), :], dst_ref=piece(kb, index),
            send_sem=ring_send, recv_sem=ring_recv.at[direction, number],
            device_id={"kb": up if direction == UP else down}, device_id_type=MESH,
        )

    def tail_place(direction, at):
        return pl.multiple_of(at * short if direction == UP else rows - (at + 1) * short, short)

    def tail_copy(direction, at, src_hop):
        block = 2 * level(direction, half - 1 + src_hop) + core
        part = w_all.at[block, :, pl.ds(tail_place(direction, at), short), :]
        return remote(
            part, part, ring_send, ring_recv.at[direction, full + at], {"kb": up if direction == UP else down}
        )

    def tail_pair(direction, at):
        part = w_all.at[2 * level(direction, half) + core, :, pl.ds(tail_place(direction, at), short), :]
        return remote(part, part, pair_send, pair_recv.at[full + at], {"kb": sibling})

    def pair(direction, number, owner):
        hop, index = number // CHUNKS + 1, place(direction, number % CHUNKS)
        block = 2 * level(direction, hop) + owner
        return pltpu.make_async_remote_copy(
            src_ref=piece(block, index), dst_ref=piece(block, index),
            send_sem=pair_send, recv_sem=pair_recv.at[number],
            device_id={"kb": sibling}, device_id_type=MESH,
        )

    def remote(src, dst, send_sem, recv_sem, device):
        return pltpu.make_async_remote_copy(
            src_ref=src, dst_ref=dst, send_sem=send_sem, recv_sem=recv_sem, device_id=device, device_id_type=MESH
        )

    def arrived(ref, sem):
        pltpu.make_async_copy(ref, ref, sem).wait()

    def own_pair(owner):
        return remote(w_hbm.at[0], w_all.at[owner], pair_send, own_recv, {"kb": sibling})

    def coef_pair(owner):
        return remote(table.at[owner], table.at[owner], coef_send, coef_pair_recv, {"kb": sibling})

    def coef_ring(direction, hop, at):
        both = table.at[pl.ds(2 * at, 2)]
        return remote(
            both, both, coef_send, coef_recv.at[direction, hop - 1], {"kb": up if direction == UP else down}
        )

    lane = lax.broadcasted_iota(jnp.int32, (1, 2 * bands), 1)
    minus_plus = jnp.where(lane < bands, -1.0, 1.0)

    def turn(block):
        return pltpu.roll(block, bands, axis=1) * minus_plus

    def make_image(size, pieces):
        rows_in = jnp.concatenate(
            [
                w_all[block, part, pl.ds(pl.multiple_of(first_row, size), size), :]
                for block, first_row, _, _ in pieces
                for part in range(2)
            ],
            axis=0,
        )
        for pair_of in range(slots // 2):
            wide = slice(pair_of * 4 * bands, (pair_of + 1) * 4 * bands)
            product = jnp.dot(rows_in, val_t[:, wide], preferred_element_type=jnp.float32)
            for i, (_, _, buffer, row) in enumerate(pieces):
                by_real = product[2 * i * size : (2 * i + 1) * size]
                by_imag = product[(2 * i + 1) * size : (2 * i + 2) * size]
                for s in range(2):
                    lanes = slice(s * 2 * bands, (s + 1) * 2 * bands)
                    to = (pair_of * 2 + s) * 2 * bands
                    image[buffer, pl.ds(pl.multiple_of(row, size), size), to : to + 2 * bands] = (
                        by_real[:, lanes] + turn(by_imag[:, lanes])
                    ).astype(jnp.bfloat16)

    def make_blocks(at, buffer):
        columns = pl.ds(pl.multiple_of(at * 2 * rows, 2 * rows), 2 * rows)
        for s in range(slots):
            acc[s] += jnp.dot(
                cond[s, :, columns],
                image[buffer, :, s * 2 * bands : (s + 1) * 2 * bands],
                preferred_element_type=jnp.float32,
            )

    loads = [
        pltpu.make_async_copy(src, dst, local_sem.at[i])
        for i, (src, dst) in enumerate((
            (coef_hbm, coef), (val_hbm, val), (w_hbm.at[0], w_all.at[kb]), (cond_hbm, cond),
            (first_hbm, first), (second_hbm, second),
        ))
    ]
    barrier = pltpu.get_barrier_semaphore()
    for other in (up, down, sibling):
        pl.semaphore_signal(barrier, inc=1, device_id={"kb": other}, device_id_type=MESH)
    for other in plane:
        pl.semaphore_signal(barrier, inc=1, device_id={"pb": other}, device_id_type=MESH)
    pl.semaphore_wait(barrier, 3 + len(plane))

    for number in range(FLIGHT):
        first_copy(UP, number).start()
        first_copy(DOWN, number).start()
    own_pair(kb).start()
    for load in loads:
        load.start()

    table[kb] = jnp.zeros_like(table[0])
    loads[0].wait()
    table[kb, 0:2, 0:local_k] = coef[...]
    coef_pair(kb).start()
    acc[...] = jnp.zeros_like(acc)
    loads[1].wait()

    def transpose(k, carry):
        columns = pl.ds(pl.multiple_of(k * 256, 256), 256)
        val_t[columns, :] = val[:, columns].T
        return carry

    lax.fori_loop(0, val.shape[1] // 256, transpose, 0)
    coef_pair(sibling).wait_recv()
    coef_ring(UP, 1, z).start()
    coef_ring(DOWN, 1, z).start()
    for load in loads[2:]:
        load.wait()
    own_pair(sibling).wait_recv()

    def step(at, carry):
        hop, index = at // CHUNKS, at % CHUNKS
        number = at - CHUNKS
        later = number + FLIGHT

        @pl.when(hop > 0)
        def _():
            for direction in (UP, DOWN):
                ring_copy(direction, number, 1).wait_recv()

                @pl.when(later < full)
                def _():
                    ring_copy(direction, later, 0).start()

                @pl.when((later >= full) & (later < full + CHUNKS // 2))
                def _():
                    for i in range(chunk // short):
                        tail_copy(direction, (later - full) * (chunk // short) + i, 0).start()

                pair(direction, number, core).start()

        @pl.when((hop > 0) & (index == 1) & (hop <= rounds_of(transfers)))
        def _():
            for other in plane:
                pl.semaphore_signal(known.at[hop - 1], inc=1, device_id={"pb": other}, device_id_type=MESH)

        @pl.when((hop > 0) & (index == CHUNKS - 1) & (hop <= rounds_of(transfers)))
        def _():
            pl.semaphore_wait(known.at[hop - 1], len(plane))

        @pl.when((hop > 0) & (index == 0))
        def _():
            coef_ring(UP, hop, level(UP, hop)).wait_recv()
            coef_ring(UP, hop + 1, level(UP, hop)).start()
            coef_ring(DOWN, hop, level(DOWN, hop)).wait_recv()

            @pl.when(hop < half - 1)
            def _():
                coef_ring(DOWN, hop + 1, level(DOWN, hop)).start()

        @pl.when(hop > 0)
        def _():
            arrived(w_all.at[pl.ds(0, 2), :, pl.ds(0, chunk), :], pair_recv.at[number])

        make_image(chunk, [
            (2 * level(direction, hop) + owner, at_row, buffer, owner * rows + at_row)
            for direction, at_row, buffer in (
                (UP, place(UP, index) * chunk, 0), (DOWN, place(DOWN, index) * chunk, jnp.where(hop > 0, 1, 0)),
            )
            for owner in range(2)
        ])

        @pl.when(index == CHUNKS - 1)
        def _():
            def blocks(buffer, carry):
                make_blocks(jnp.where(buffer == 0, level(UP, hop), level(DOWN, hop)), buffer)
                return carry

            lax.fori_loop(0, jnp.where(hop > 0, 2, 1), blocks, 0)

        return carry

    lax.fori_loop(CHUNKS // 2, half * CHUNKS, step, 0)

    coef_ring(UP, half, level(UP, half)).wait_recv()
    where_block = lax.broadcasted_iota(jnp.int32, table.shape, 0)
    where_lane = lax.broadcasted_iota(jnp.int32, table.shape, 2)
    point = jnp.where(where_lane < local_k, where_block * local_k + where_lane, -1)
    coefs = table[...]
    for s in range(slots):
        chosen = jnp.sum(jnp.where(point == second[0, s], coefs, 0.0), axis=0)
        chosen = jnp.sum(chosen, axis=1, keepdims=True)
        picked[2 * s : 2 * s + 2, :] = jnp.broadcast_to(chosen[0:2, :], (2, picked.shape[1]))

    def last_step(at, carry):
        for direction in (UP, DOWN):
            tail_copy(direction, at, 1).wait_recv()
            tail_pair(direction, at).start()
        arrived(w_all.at[pl.ds(0, 2), :, pl.ds(0, short), :], pair_recv.at[full + at])
        make_image(short, [
            (2 * level(UP, half) + owner, at_row, 0, owner * rows + at_row)
            for at_row in (tail_place(UP, at), tail_place(DOWN, at))
            for owner in range(2)
        ])
        return carry

    lax.fori_loop(0, TAIL, last_step, 0)
    make_blocks(level(UP, half), 0)

    totals = [jnp.zeros((bands, 2 * bands), jnp.float32) for _ in range(local_k)]
    for s in range(slots):
        block = acc[s, 0:bands, :] - turn(acc[s, bands:, :])
        term = block * picked[2 * s : 2 * s + 1, :] + turn(block) * picked[2 * s + 1 : 2 * s + 2, :]
        owner = first[0, s] - kb * local_k
        for k in range(local_k):
            totals[k] += jnp.where(owner == k, term, 0.0)
    take = bands // transfers
    for k in range(local_k):
        for to in range(transfers):
            stage[to, k * take : (k + 1) * take, :] = totals[k][to * take : (to + 1) * take, :]
    for i, distance in enumerate(far_first):
        to = lax.rem(pb + distance, transfers)
        remote(stage.at[to], landed.at[i], sum_send, sum_recv, {"pb": to}).start()
    arrived(w_all.at[pl.ds(0, ring - 1)], ring_send)
    arrived(w_all.at[pl.ds(0, ring)], pair_send)
    arrived(table.at[pl.ds(0, 1 + 2 * (2 * half - 1))], coef_send)
    total = stage[pb]
    arrived(landed.at[pl.ds(0, transfers - 1)], sum_recv)
    for i in range(transfers - 1):
        total += landed[i]
    for k in range(local_k):
        for i in range(take // 2):
            even = total[k * take + 2 * i : k * take + 2 * i + 1, :]
            odd = total[k * take + 2 * i + 1 : k * take + 2 * i + 2, :]
            lanes = slice(i * 2 * bands, (i + 1) * 2 * bands)
            out_ref[k, 0:1, lanes] = jnp.where(lane < bands, even, pltpu.roll(odd, bands, axis=1))
            out_ref[k, 1:2, lanes] = jnp.where(lane < bands, pltpu.roll(even, bands, axis=1), odd)
    arrived(landed.at[pl.ds(0, transfers - 1)], sum_send)


def body(ring, transfers, screened, elem_val, elem_cond, pair_first, pair_second, coeffs):
    slots, _, _, bands, depth = elem_val.shape
    rows = screened.shape[2]
    local_k = coeffs.shape[0]
    half = ring // 2
    take = bands // transfers
    dma = pltpu.SemaphoreType.DMA
    width = slots * 2 * bands
    return pl.pallas_call(
        functools.partial(kernel, ring, transfers),
        out_shape=jax.ShapeDtypeStruct((local_k, 2, take * bands), jnp.float32),
        in_specs=[pl.BlockSpec(memory_space=pltpu.HBM)] * 6,
        out_specs=pl.BlockSpec(memory_space=pltpu.VMEM),
        scratch_shapes=[
            pltpu.VMEM((2 * ring, 2, rows, depth), jnp.bfloat16),
            pltpu.VMEM((width, depth), jnp.bfloat16),
            pltpu.VMEM((depth, width), jnp.bfloat16),
            pltpu.VMEM((slots, 2 * bands, depth), jnp.bfloat16),
            pltpu.VMEM((2, 2 * rows, width), jnp.bfloat16),
            pltpu.VMEM((slots, 2 * bands, 2 * bands), jnp.float32),
            pltpu.VMEM((2 * ring, 8, 128), jnp.float32),
            pltpu.VMEM((2 * slots, 128), jnp.float32),
            pltpu.VMEM((transfers, local_k * take, 2 * bands), jnp.float32),
            pltpu.VMEM((transfers, local_k * take, 2 * bands), jnp.float32),
            pltpu.SMEM((1, slots), jnp.int32),
            pltpu.SMEM((1, slots), jnp.int32),
            pltpu.VMEM((2, local_k), jnp.float32),
            dma((6,)),
            dma(()),
            dma((2, (half - 1) * CHUNKS + TAIL)),
            dma(()),
            dma(((half - 1) * CHUNKS + TAIL,)),
            dma(()),
            dma(()),
            dma((2, half)),
            dma(()),
            dma(()),
            dma(()),
            pltpu.SemaphoreType.REGULAR((rounds_of(transfers),)),
        ],
        compiler_params=pltpu.CompilerParams(
            collective_id=0, has_side_effects=True, vmem_limit_bytes=40 * 1024 * 1024
        ),
        cost_estimate=pl.CostEstimate(
            flops=8 * depth * depth * slots * bands, bytes_accessed=8 * 1024 * 1024, transcendentals=0
        ),
    )(*(
        pltpu.with_memory_space_constraint(operand, pltpu.HBM)
        for operand in (
            screened, elem_val.reshape(width, depth), elem_cond.reshape(slots, 2 * bands, depth),
            pair_first.T, pair_second.T, coeffs.T,
        )
    ))


def solution(mesh):
    in_specs = (
        P("pb", None, "kb", None),
        P("kb", "pb", None, None, None),
        P("kb", "pb", None, None, None),
        P("kb", "pb"),
        P("kb", "pb"),
        P("kb", None),
    )
    out_specs = P("kb", None, "pb")
    ring, transfers = mesh.shape["kb"] // 2, mesh.shape["pb"]
    return jax.shard_map(
        functools.partial(body, ring, transfers), mesh=mesh, in_specs=in_specs, out_specs=out_specs, check_vma=False
    )
```

```python
import functools

import jax
import jax.numpy as jnp
from jax import lax
from jax.experimental import pallas as pl
from jax.experimental.pallas import tpu as pltpu
from jax.sharding import PartitionSpec as P

MESH = pl.DeviceIdType.MESH
CHUNKS = 4
FLIGHT = 2
TAIL = 4
DIRECT = 4
UP, DOWN = 0, 1


def side_of(transfers):
    return 1 << ((transfers.bit_length() - 1) // 2)


def rounds_of(ring, transfers):
    side = side_of(transfers)
    return 2 * (ring // 2) + side // 2 + transfers // side // 2 - 1


def kernel(
    ring, transfers, w_hbm, val_hbm, cond_hbm, first_hbm, second_hbm, coef_hbm, out_ref,
    w_all, val, val_t, cond, image, acc, table, picked, stage, landed, first, second, coef,
    local_sem, ring_send, ring_recv, pair_send, pair_recv, own_recv, tail_send, tail_pair_send, end_send, end_recv,
    coef_send, coef_recv, coef_pair_recv, sum_send, sum_recv, known, joined,
):
    half = ring // 2
    rows = w_hbm.shape[2]
    chunk = rows // CHUNKS
    slots = cond.shape[0]
    local_k = coef.shape[1]
    bands = cond.shape[1] // 2
    full = (half - 1) * CHUNKS
    short = rows // 2 // TAIL
    kb, pb = lax.axis_index("kb"), lax.axis_index("pb")
    z, core = kb // 2, kb % 2
    sibling = kb + 1 - 2 * core
    up = lax.rem(z + 1, ring) * 2 + core
    down = lax.rem(z + ring - 1, ring) * 2 + core

    side = side_of(transfers)
    y, x = pb // side, pb % side
    tall = transfers // side

    def hops(dy, dx):
        return min(dy, tall - dy) + min(dx, side - dx)

    others = sorted(
        ((dy, dx) for dy in range(tall) for dx in range(side) if dy or dx), key=lambda by: -hops(*by)
    )
    others = [(lax.rem(y + dy, tall) * side + lax.rem(x + dx, side), hops(dy, dx)) for dy, dx in others]
    plane = [other for other, far in others if far == 1]

    rounds = rounds_of(ring, transfers)

    def tell(number):
        for other in (up, down):
            pl.semaphore_signal(known.at[number % 2], inc=1, device_id={"kb": other}, device_id_type=MESH)

        @pl.when(z == 0)
        def _():
            for other in plane:
                pl.semaphore_signal(known.at[number % 2], inc=1, device_id={"pb": other}, device_id_type=MESH)

    def hear(number):
        pl.semaphore_wait(known.at[number % 2], jnp.where(z == 0, 2 + len(plane), 2))

    def level(direction, hop):
        return lax.rem(z + ring - hop, ring) if direction == UP else lax.rem(z + hop, ring)

    def place(direction, index):
        return index if direction == UP else CHUNKS - 1 - index

    def piece(block, index):
        return w_all.at[block, :, pl.ds(pl.multiple_of(index * chunk, chunk), chunk), :]

    def ring_copy(direction, number, src_hop):
        hop, index = number // CHUNKS + src_hop, place(direction, number % CHUNKS)
        block = 2 * level(direction, hop) + core
        return pltpu.make_async_remote_copy(
            src_ref=piece(block, index), dst_ref=piece(block, index),
            send_sem=ring_send, recv_sem=ring_recv.at[direction, number],
            device_id={"kb": up if direction == UP else down}, device_id_type=MESH,
        )

    def first_copy(direction, number):
        index = place(direction, number)
        return pltpu.make_async_remote_copy(
            src_ref=w_hbm.at[0, :, pl.ds(index * chunk, chunk), :], dst_ref=piece(kb, index),
            send_sem=ring_send, recv_sem=ring_recv.at[direction, number],
            device_id={"kb": up if direction == UP else down}, device_id_type=MESH,
        )

    def tail_place(direction, at):
        return pl.multiple_of(at * short if direction == UP else rows - (at + 1) * short, short)

    depth = w_hbm.shape[3]
    shared = depth - depth // DIRECT

    def tail_copy(direction, at, src_hop, lanes=depth, send_sem=tail_send.at[0]):
        block = 2 * level(direction, half - 1 + src_hop) + core
        part = w_all.at[block, :, pl.ds(tail_place(direction, at), short), pl.ds(0, lanes)]
        return remote(
            part, part, send_sem, ring_recv.at[direction, full + at], {"kb": up if direction == UP else down}
        )

    def tail_pair(direction, at, lanes=depth, send_sem=tail_pair_send.at[0]):
        block = 2 * level(direction, half) + core
        part = w_all.at[block, :, pl.ds(tail_place(direction, at), short), pl.ds(0, lanes)]
        return remote(part, part, send_sem, pair_recv.at[full + at], {"kb": sibling})

    def end_copy(direction, to_core):
        block = 2 * level(direction, half - 1) + core
        part = w_all.at[block, :, pl.ds(tail_place(direction, TAIL - 1), short), pl.ds(shared, depth - shared)]
        chip = up - core if direction == UP else down - core
        return remote(part, part, end_send, end_recv, {"kb": chip + to_core})

    def pair(direction, number, owner):
        hop, index = number // CHUNKS + 1, place(direction, number % CHUNKS)
        block = 2 * level(direction, hop) + owner
        return pltpu.make_async_remote_copy(
            src_ref=piece(block, index), dst_ref=piece(block, index),
            send_sem=pair_send, recv_sem=pair_recv.at[number],
            device_id={"kb": sibling}, device_id_type=MESH,
        )

    def remote(src, dst, send_sem, recv_sem, device):
        return pltpu.make_async_remote_copy(
            src_ref=src, dst_ref=dst, send_sem=send_sem, recv_sem=recv_sem, device_id=device, device_id_type=MESH
        )

    def arrived(ref, sem):
        pltpu.make_async_copy(ref, ref, sem).wait()

    def own_pair(owner):
        return remote(w_hbm.at[0], w_all.at[owner], pair_send, own_recv, {"kb": sibling})

    def coef_pair(owner):
        return remote(table.at[owner], table.at[owner], coef_send, coef_pair_recv, {"kb": sibling})

    def coef_ring(direction, hop, at):
        both = table.at[pl.ds(2 * at, 2)]
        return remote(
            both, both, coef_send, coef_recv.at[direction, hop - 1], {"kb": up if direction == UP else down}
        )

    lane = lax.broadcasted_iota(jnp.int32, (1, 2 * bands), 1)
    minus_plus = jnp.where(lane < bands, -1.0, 1.0)

    def turn(block):
        return pltpu.roll(block, bands, axis=1) * minus_plus

    def make_image(size, pieces):
        rows_in = jnp.concatenate(
            [
                w_all[block, part, pl.ds(pl.multiple_of(first_row, size), size), :]
                for block, first_row, _, _ in pieces
                for part in range(2)
            ],
            axis=0,
        )
        for pair_of in range(slots // 2):
            wide = slice(pair_of * 4 * bands, (pair_of + 1) * 4 * bands)
            product = jnp.dot(rows_in, val_t[:, wide], preferred_element_type=jnp.float32)
            for i, (_, _, buffer, row) in enumerate(pieces):
                by_real = product[2 * i * size : (2 * i + 1) * size]
                by_imag = product[(2 * i + 1) * size : (2 * i + 2) * size]
                for s in range(2):
                    lanes = slice(s * 2 * bands, (s + 1) * 2 * bands)
                    to = (pair_of * 2 + s) * 2 * bands
                    image[buffer, pl.ds(pl.multiple_of(row, size), size), to : to + 2 * bands] = (
                        by_real[:, lanes] + turn(by_imag[:, lanes])
                    ).astype(jnp.bfloat16)

    def make_blocks(at, buffer):
        columns = pl.ds(pl.multiple_of(at * 2 * rows, 2 * rows), 2 * rows)
        for s in range(slots):
            acc[s] += jnp.dot(
                cond[s, :, columns],
                image[buffer, :, s * 2 * bands : (s + 1) * 2 * bands],
                preferred_element_type=jnp.float32,
            )

    loads = [
        pltpu.make_async_copy(src, dst, local_sem.at[i])
        for i, (src, dst) in enumerate((
            (coef_hbm, coef), (val_hbm, val), (w_hbm.at[0], w_all.at[kb]), (cond_hbm, cond),
            (first_hbm, first), (second_hbm, second),
        ))
    ]
    barrier = pltpu.get_barrier_semaphore()
    for other in (down, sibling):
        pl.semaphore_signal(barrier, inc=1, device_id={"kb": other}, device_id_type=MESH)

    @pl.when(z == 0)
    def _():
        for other in plane:
            pl.semaphore_signal(barrier, inc=1, device_id={"pb": other}, device_id_type=MESH)

    pl.semaphore_wait(barrier, jnp.where(z == 0, 2 + len(plane), 2))

    pl.semaphore_signal(joined, inc=1, device_id={"kb": up}, device_id_type=MESH)
    for number in range(FLIGHT):
        first_copy(UP, number).start()
    own_pair(kb).start()
    for load in loads:
        load.start()
    pl.semaphore_wait(joined, 1)
    for number in range(FLIGHT):
        first_copy(DOWN, number).start()

    table[kb] = jnp.zeros_like(table[0])
    loads[0].wait()
    table[kb, 0:2, 0:local_k] = coef[...]
    coef_pair(kb).start()
    acc[...] = jnp.zeros_like(acc)
    loads[1].wait()

    def transpose(k, carry):
        columns = pl.ds(pl.multiple_of(k * 256, 256), 256)
        val_t[columns, :] = val[:, columns].T
        return carry

    lax.fori_loop(0, val.shape[1] // 256, transpose, 0)
    coef_pair(sibling).wait_recv()
    coef_ring(UP, 1, z).start()
    coef_ring(DOWN, 1, z).start()
    for load in loads[2:]:
        load.wait()
    own_pair(sibling).wait_recv()

    def step(at, carry):
        hop, index = at // CHUNKS, at % CHUNKS
        number = at - CHUNKS
        later = number + FLIGHT

        @pl.when(hop > 0)
        def _():
            for direction in (UP, DOWN):
                ring_copy(direction, number, 1).wait_recv()

                @pl.when(later < full)
                def _():
                    ring_copy(direction, later, 0).start()

                @pl.when((later >= full) & (later < full + CHUNKS // 2))
                def _():
                    for i in range(chunk // short):
                        piece_at = (later - full) * (chunk // short) + i

                        @pl.when(piece_at < TAIL - 1)
                        def _():
                            tail_copy(direction, piece_at, 0).start()

                @pl.when(later == full + CHUNKS // 2 - 1)
                def _():
                    tail_copy(direction, TAIL - 1, 0, shared, tail_send.at[1]).start()
                    end_copy(direction, core).start()
                    end_copy(direction, 1 - core).start()

                pair(direction, number, core).start()

        @pl.when((number > 0) & (number <= rounds))
        def _():
            hear(number - 1)

        @pl.when((number >= 0) & (number < rounds))
        def _():
            tell(number)

        @pl.when((hop > 0) & (index == 0))
        def _():
            coef_ring(UP, hop, level(UP, hop)).wait_recv()
            coef_ring(UP, hop + 1, level(UP, hop)).start()
            coef_ring(DOWN, hop, level(DOWN, hop)).wait_recv()

            @pl.when(hop < half - 1)
            def _():
                coef_ring(DOWN, hop + 1, level(DOWN, hop)).start()

        @pl.when(hop > 0)
        def _():
            arrived(w_all.at[pl.ds(0, 2), :, pl.ds(0, chunk), :], pair_recv.at[number])

        make_image(chunk, [
            (2 * level(direction, hop) + owner, at_row, buffer, owner * rows + at_row)
            for direction, at_row, buffer in (
                (UP, place(UP, index) * chunk, 0), (DOWN, place(DOWN, index) * chunk, jnp.where(hop > 0, 1, 0)),
            )
            for owner in range(2)
        ])

        @pl.when(index == CHUNKS - 1)
        def _():
            def blocks(buffer, carry):
                make_blocks(jnp.where(buffer == 0, level(UP, hop), level(DOWN, hop)), buffer)
                return carry

            lax.fori_loop(0, jnp.where(hop > 0, 2, 1), blocks, 0)

        return carry

    lax.fori_loop(CHUNKS // 2, half * CHUNKS, step, 0)
    for number in range(full, rounds + 1):
        hear(number - 1)
        if number < rounds:
            tell(number)

    coef_ring(UP, half, level(UP, half)).wait_recv()
    where_block = lax.broadcasted_iota(jnp.int32, table.shape, 0)
    where_lane = lax.broadcasted_iota(jnp.int32, table.shape, 2)
    point = jnp.where(where_lane < local_k, where_block * local_k + where_lane, -1)
    coefs = table[...]
    for s in range(slots):
        chosen = jnp.sum(jnp.where(point == second[0, s], coefs, 0.0), axis=0)
        chosen = jnp.sum(chosen, axis=1, keepdims=True)
        picked[2 * s : 2 * s + 2, :] = jnp.broadcast_to(chosen[0:2, :], (2, picked.shape[1]))

    def last_step(at, carry):
        @pl.when(at < TAIL - 1)
        def _():
            for direction in (UP, DOWN):
                tail_copy(direction, at, 1).wait_recv()
                tail_pair(direction, at).start()
            arrived(w_all.at[pl.ds(0, 2), :, pl.ds(0, short), :], pair_recv.at[full + at])

        @pl.when(at == TAIL - 1)
        def _():
            for direction in (UP, DOWN):
                tail_copy(direction, TAIL - 1, 1, shared).wait_recv()
                tail_pair(direction, TAIL - 1, shared, tail_pair_send.at[1]).start()
            arrived(w_all.at[pl.ds(0, 2), :, pl.ds(0, short), pl.ds(0, shared)], pair_recv.at[full + TAIL - 1])
            arrived(w_all.at[pl.ds(0, 4), :, pl.ds(0, short), pl.ds(0, depth - shared)], end_recv)

        make_image(short, [
            (2 * level(UP, half) + owner, at_row, 0, owner * rows + at_row)
            for at_row in (tail_place(UP, at), tail_place(DOWN, at))
            for owner in range(2)
        ])
        return carry

    lax.fori_loop(0, TAIL, last_step, 0)
    make_blocks(level(UP, half), 0)

    totals = [jnp.zeros((bands, 2 * bands), jnp.float32) for _ in range(local_k)]
    for s in range(slots):
        block = acc[s, 0:bands, :] - turn(acc[s, bands:, :])
        term = block * picked[2 * s : 2 * s + 1, :] + turn(block) * picked[2 * s + 1 : 2 * s + 2, :]
        owner = first[0, s] - kb * local_k
        for k in range(local_k):
            totals[k] += jnp.where(owner == k, term, 0.0)
    take = bands // transfers
    for k in range(local_k):
        for to in range(transfers):
            stage[to, k * take : (k + 1) * take, :] = totals[k][to * take : (to + 1) * take, :]
    for i, (to, _) in enumerate(others):
        remote(stage.at[to], landed.at[i], sum_send, sum_recv, {"pb": to}).start()
    arrived(w_all.at[pl.ds(0, ring - 2)], ring_send)
    arrived(w_all.at[pl.ds(0, ring - 1)], pair_send)
    for sent in (tail_send, tail_pair_send):
        arrived(w_all.at[0, :, pl.ds(0, 2 * (TAIL - 1) * short), :], sent.at[0])
        arrived(w_all.at[0, :, pl.ds(0, 2 * short), pl.ds(0, shared)], sent.at[1])
    arrived(w_all.at[pl.ds(0, 4), :, pl.ds(0, short), pl.ds(0, depth - shared)], end_send)
    arrived(table.at[pl.ds(0, 1 + 2 * (2 * half - 1))], coef_send)
    total = stage[pb]
    arrived(landed.at[pl.ds(0, transfers - 1)], sum_recv)
    for i in range(transfers - 1):
        total += landed[i]
    for k in range(local_k):
        for i in range(take // 2):
            even = total[k * take + 2 * i : k * take + 2 * i + 1, :]
            odd = total[k * take + 2 * i + 1 : k * take + 2 * i + 2, :]
            lanes = slice(i * 2 * bands, (i + 1) * 2 * bands)
            out_ref[k, 0:1, lanes] = jnp.where(lane < bands, even, pltpu.roll(odd, bands, axis=1))
            out_ref[k, 1:2, lanes] = jnp.where(lane < bands, pltpu.roll(even, bands, axis=1), odd)
    arrived(landed.at[pl.ds(0, transfers - 1)], sum_send)


def body(ring, transfers, screened, elem_val, elem_cond, pair_first, pair_second, coeffs):
    slots, _, _, bands, depth = elem_val.shape
    rows = screened.shape[2]
    local_k = coeffs.shape[0]
    half = ring // 2
    take = bands // transfers
    dma = pltpu.SemaphoreType.DMA
    width = slots * 2 * bands
    return pl.pallas_call(
        functools.partial(kernel, ring, transfers),
        out_shape=jax.ShapeDtypeStruct((local_k, 2, take * bands), jnp.float32),
        in_specs=[pl.BlockSpec(memory_space=pltpu.HBM)] * 6,
        out_specs=pl.BlockSpec(memory_space=pltpu.VMEM),
        scratch_shapes=[
            pltpu.VMEM((2 * ring, 2, rows, depth), jnp.bfloat16),
            pltpu.VMEM((width, depth), jnp.bfloat16),
            pltpu.VMEM((depth, width), jnp.bfloat16),
            pltpu.VMEM((slots, 2 * bands, depth), jnp.bfloat16),
            pltpu.VMEM((2, 2 * rows, width), jnp.bfloat16),
            pltpu.VMEM((slots, 2 * bands, 2 * bands), jnp.float32),
            pltpu.VMEM((2 * ring, 8, 128), jnp.float32),
            pltpu.VMEM((2 * slots, 128), jnp.float32),
            pltpu.VMEM((transfers, local_k * take, 2 * bands), jnp.float32),
            pltpu.VMEM((transfers, local_k * take, 2 * bands), jnp.float32),
            pltpu.SMEM((1, slots), jnp.int32),
            pltpu.SMEM((1, slots), jnp.int32),
            pltpu.VMEM((2, local_k), jnp.float32),
            dma((6,)),
            dma(()),
            dma((2, (half - 1) * CHUNKS + TAIL)),
            dma(()),
            dma(((half - 1) * CHUNKS + TAIL,)),
            dma(()),
            dma((2,)),
            dma((2,)),
            dma(()),
            dma(()),
            dma(()),
            dma((2, half)),
            dma(()),
            dma(()),
            dma(()),
            pltpu.SemaphoreType.REGULAR((2,)),
            pltpu.SemaphoreType.REGULAR,
        ],
        compiler_params=pltpu.CompilerParams(
            collective_id=0, has_side_effects=True, vmem_limit_bytes=40 * 1024 * 1024
        ),
        cost_estimate=pl.CostEstimate(
            flops=8 * depth * depth * slots * bands, bytes_accessed=8 * 1024 * 1024, transcendentals=0
        ),
    )(*(
        pltpu.with_memory_space_constraint(operand, pltpu.HBM)
        for operand in (
            screened, elem_val.reshape(width, depth), elem_cond.reshape(slots, 2 * bands, depth),
            pair_first.T, pair_second.T, coeffs.T,
        )
    ))


def solution(mesh):
    in_specs = (
        P("pb", None, "kb", None),
        P("kb", "pb", None, None, None),
        P("kb", "pb", None, None, None),
        P("kb", "pb"),
        P("kb", "pb"),
        P("kb", None),
    )
    out_specs = P("kb", None, "pb")
    ring, transfers = mesh.shape["kb"] // 2, mesh.shape["pb"]
    return jax.shard_map(
        functools.partial(body, ring, transfers), mesh=mesh, in_specs=in_specs, out_specs=out_specs, check_vma=False
    )
```

```python
import functools

import jax
import jax.numpy as jnp
from jax import lax
from jax.experimental import pallas as pl
from jax.experimental.pallas import tpu as pltpu
from jax.sharding import PartitionSpec as P

MESH = pl.DeviceIdType.MESH
CHUNKS = 4
FLIGHT = 2
TAIL = 4
REUSE = 6
DIRECT = 4
UP, DOWN = 0, 1


def side_of(transfers):
    return 1 << ((transfers.bit_length() - 1) // 2)


def rounds_of(ring, transfers):
    side = side_of(transfers)
    return 2 * (ring // 2) + side // 2 + transfers // side // 2 - 1


def kernel(
    ring, transfers, w_hbm, val_hbm, cond_hbm, first_hbm, second_hbm, coef_hbm, out_ref,
    w_all, val, val_t, cond, image, acc, table, picked, stage, landed, first, second, coef,
    local_sem, ring_send, ring_recv, pair_send, pair_recv, own_recv, tail_send, tail_pair_send, end_send, end_recv,
    coef_send, coef_recv, coef_pair_recv, sum_send, sum_recv, known, joined,
):
    half = ring // 2
    rows = w_hbm.shape[2]
    chunk = rows // CHUNKS
    slots = cond.shape[0]
    local_k = coef.shape[1]
    bands = cond.shape[1] // 2
    full = (half - 1) * CHUNKS
    short = rows // 2 // TAIL
    kb, pb = lax.axis_index("kb"), lax.axis_index("pb")
    z, core = kb // 2, kb % 2
    sibling = kb + 1 - 2 * core
    up = lax.rem(z + 1, ring) * 2 + core
    down = lax.rem(z + ring - 1, ring) * 2 + core

    side = side_of(transfers)
    y, x = pb // side, pb % side
    tall = transfers // side

    def hops(dy, dx):
        return min(dy, tall - dy) + min(dx, side - dx)

    others = sorted(
        ((dy, dx) for dy in range(tall) for dx in range(side) if dy or dx), key=lambda by: -hops(*by)
    )
    others = [(lax.rem(y + dy, tall) * side + lax.rem(x + dx, side), hops(dy, dx)) for dy, dx in others]
    plane = [other for other, far in others if far == 1]

    rounds = rounds_of(ring, transfers)

    def tell(number):
        for other in (up, down):
            pl.semaphore_signal(known.at[number % 2], inc=1, device_id={"kb": other}, device_id_type=MESH)

        @pl.when(z == 0)
        def _():
            for other in plane:
                pl.semaphore_signal(known.at[number % 2], inc=1, device_id={"pb": other}, device_id_type=MESH)

    def hear(number):
        pl.semaphore_wait(known.at[number % 2], jnp.where(z == 0, 2 + len(plane), 2))

    def level(direction, hop):
        return lax.rem(z + ring - hop, ring) if direction == UP else lax.rem(z + hop, ring)

    def place(direction, index):
        return index if direction == UP else CHUNKS - 1 - index

    def piece(block, index):
        return w_all.at[block, :, pl.ds(pl.multiple_of(index * chunk, chunk), chunk), :]

    def ring_copy(direction, number, src_hop):
        hop, index = number // CHUNKS + src_hop, place(direction, number % CHUNKS)
        block = 2 * level(direction, hop) + core
        return pltpu.make_async_remote_copy(
            src_ref=piece(block, index), dst_ref=piece(block, index),
            send_sem=ring_send, recv_sem=ring_recv.at[direction, number % REUSE],
            device_id={"kb": up if direction == UP else down}, device_id_type=MESH,
        )

    def first_copy(direction, number):
        index = place(direction, number)
        return pltpu.make_async_remote_copy(
            src_ref=w_hbm.at[0, :, pl.ds(index * chunk, chunk), :], dst_ref=piece(kb, index),
            send_sem=ring_send, recv_sem=ring_recv.at[direction, number % REUSE],
            device_id={"kb": up if direction == UP else down}, device_id_type=MESH,
        )

    def tail_place(direction, at):
        return pl.multiple_of(at * short if direction == UP else rows - (at + 1) * short, short)

    depth = w_hbm.shape[3]
    shared = depth - depth // DIRECT

    def tail_copy(direction, at, src_hop, lanes=depth, send_sem=tail_send.at[0]):
        block = 2 * level(direction, half - 1 + src_hop) + core
        part = w_all.at[block, :, pl.ds(tail_place(direction, at), short), pl.ds(0, lanes)]
        return remote(
            part, part, send_sem, ring_recv.at[direction, REUSE + at], {"kb": up if direction == UP else down}
        )

    def tail_pair(direction, at, lanes=depth, send_sem=tail_pair_send.at[0]):
        block = 2 * level(direction, half) + core
        part = w_all.at[block, :, pl.ds(tail_place(direction, at), short), pl.ds(0, lanes)]
        return remote(part, part, send_sem, pair_recv.at[(full + at) % 2], {"kb": sibling})

    def end_copy(direction, by, to_core):
        block = 2 * level(by, half - 1) + core
        part = w_all.at[block, :, pl.ds(tail_place(direction, TAIL - 1), short), pl.ds(shared, depth - shared)]
        chip = up - core if by == UP else down - core
        return remote(part, part, end_send.at[direction], end_recv, {"kb": chip + to_core})

    end_less, end_more = z == ring - 1, z == 1

    def pair(direction, number, owner):
        hop, index = number // CHUNKS + 1, place(direction, number % CHUNKS)
        block = 2 * level(direction, hop) + owner
        return pltpu.make_async_remote_copy(
            src_ref=piece(block, index), dst_ref=piece(block, index),
            send_sem=pair_send, recv_sem=pair_recv.at[number % 2],
            device_id={"kb": sibling}, device_id_type=MESH,
        )

    def remote(src, dst, send_sem, recv_sem, device):
        return pltpu.make_async_remote_copy(
            src_ref=src, dst_ref=dst, send_sem=send_sem, recv_sem=recv_sem, device_id=device, device_id_type=MESH
        )

    def arrived(ref, sem):
        pltpu.make_async_copy(ref, ref, sem).wait()

    def own_pair(owner):
        return remote(w_hbm.at[0], w_all.at[owner], pair_send, own_recv, {"kb": sibling})

    def coef_pair(owner):
        return remote(table.at[owner], table.at[owner], coef_send, coef_pair_recv, {"kb": sibling})

    def coef_ring(direction, hop, at):
        both = table.at[pl.ds(2 * at, 2)]
        return remote(
            both, both, coef_send, coef_recv.at[direction, hop - 1], {"kb": up if direction == UP else down}
        )

    lane = lax.broadcasted_iota(jnp.int32, (1, 2 * bands), 1)
    minus_plus = jnp.where(lane < bands, -1.0, 1.0)

    def turn(block):
        return pltpu.roll(block, bands, axis=1) * minus_plus

    def make_image(size, pieces):
        rows_in = jnp.concatenate(
            [
                w_all[block, part, pl.ds(pl.multiple_of(first_row, size), size), :]
                for block, first_row, _, _ in pieces
                for part in range(2)
            ],
            axis=0,
        )
        for pair_of in range(slots // 2):
            wide = slice(pair_of * 4 * bands, (pair_of + 1) * 4 * bands)
            product = jnp.dot(rows_in, val_t[:, wide], preferred_element_type=jnp.float32)
            for i, (_, _, buffer, row) in enumerate(pieces):
                by_real = product[2 * i * size : (2 * i + 1) * size]
                by_imag = product[(2 * i + 1) * size : (2 * i + 2) * size]
                for s in range(2):
                    lanes = slice(s * 2 * bands, (s + 1) * 2 * bands)
                    to = (pair_of * 2 + s) * 2 * bands
                    image[buffer, pl.ds(pl.multiple_of(row, size), size), to : to + 2 * bands] = (
                        by_real[:, lanes] + turn(by_imag[:, lanes])
                    ).astype(jnp.bfloat16)

    def make_blocks(at, buffer):
        columns = pl.ds(pl.multiple_of(at * 2 * rows, 2 * rows), 2 * rows)
        for s in range(slots):
            acc[s] += jnp.dot(
                cond[s, :, columns],
                image[buffer, :, s * 2 * bands : (s + 1) * 2 * bands],
                preferred_element_type=jnp.float32,
            )

    loads = [
        pltpu.make_async_copy(src, dst, local_sem.at[i])
        for i, (src, dst) in enumerate((
            (coef_hbm, coef), (val_hbm, val), (w_hbm.at[0], w_all.at[kb]), (cond_hbm, cond),
            (first_hbm, first), (second_hbm, second),
        ))
    ]
    barrier = pltpu.get_barrier_semaphore()

    def first_out(direction):
        for number in range(FLIGHT):
            first_copy(direction, number).start()

    above_is_nearer, below_is_nearer = z >= half, (z > 0) & (z <= half)

    @pl.when(jnp.logical_not(above_is_nearer))
    def _():
        pl.semaphore_signal(barrier, inc=1, device_id={"kb": up}, device_id_type=MESH)

    @pl.when(jnp.logical_not(below_is_nearer))
    def _():
        pl.semaphore_signal(barrier, inc=1, device_id={"kb": down}, device_id_type=MESH)

    pl.semaphore_signal(barrier, inc=1, device_id={"kb": sibling}, device_id_type=MESH)

    @pl.when(z == 0)
    def _():
        for other in plane:
            pl.semaphore_signal(barrier, inc=1, device_id={"pb": other}, device_id_type=MESH)

    pl.semaphore_wait(barrier, jnp.where(z == 0, 1 + len(plane), jnp.where(z == half, 3, 2)))

    @pl.when(above_is_nearer)
    def _():
        pl.semaphore_signal(joined.at[DOWN], inc=1, device_id={"kb": up}, device_id_type=MESH)
        first_out(UP)

    @pl.when(below_is_nearer)
    def _():
        pl.semaphore_signal(joined.at[UP], inc=1, device_id={"kb": down}, device_id_type=MESH)
        first_out(DOWN)

    own_pair(kb).start()
    for load in loads:
        load.start()

    @pl.when(jnp.logical_not(above_is_nearer))
    def _():
        pl.semaphore_wait(joined.at[UP], 1)
        first_out(UP)

    @pl.when(jnp.logical_not(below_is_nearer))
    def _():
        pl.semaphore_wait(joined.at[DOWN], 1)
        first_out(DOWN)

    table[kb] = jnp.zeros_like(table[0])
    loads[0].wait()
    table[kb, 0:2, 0:local_k] = coef[...]
    coef_pair(kb).start()
    acc[...] = jnp.zeros_like(acc)
    loads[1].wait()

    def transpose(k, carry):
        columns = pl.ds(pl.multiple_of(k * 256, 256), 256)
        val_t[columns, :] = val[:, columns].T
        return carry

    lax.fori_loop(0, val.shape[1] // 256, transpose, 0)
    coef_pair(sibling).wait_recv()
    coef_ring(UP, 1, z).start()
    coef_ring(DOWN, 1, z).start()
    for load in loads[2:]:
        load.wait()
    own_pair(sibling).wait_recv()

    def step(at, carry):
        hop, index = at // CHUNKS, at % CHUNKS
        number = at - CHUNKS
        later = number + FLIGHT

        @pl.when(hop > 0)
        def _():
            for direction in (UP, DOWN):
                ring_copy(direction, number, 1).wait_recv()

                @pl.when(later < full)
                def _():
                    ring_copy(direction, later, 0).start()

                @pl.when(later == full)
                def _():
                    tail_copy(direction, 0, 0).start()

                @pl.when(later == full + 1)
                def _():
                    for at in range(1, TAIL - 1):
                        tail_copy(direction, at, 0).start()

                pair(direction, number, core).start()

        @pl.when((number > 0) & (number <= rounds))
        def _():
            hear(number - 1)

        @pl.when((number >= 0) & (number < rounds))
        def _():
            tell(number)

        @pl.when((hop > 0) & (index == 0))
        def _():
            coef_ring(UP, hop, level(UP, hop)).wait_recv()
            coef_ring(UP, hop + 1, level(UP, hop)).start()
            coef_ring(DOWN, hop, level(DOWN, hop)).wait_recv()

            @pl.when(hop < half - 1)
            def _():
                coef_ring(DOWN, hop + 1, level(DOWN, hop)).start()

        @pl.when(hop > 0)
        def _():
            arrived(w_all.at[pl.ds(0, 2), :, pl.ds(0, chunk), :], pair_recv.at[number % 2])

        make_image(chunk, [
            (2 * level(direction, hop) + owner, at_row, buffer, owner * rows + at_row)
            for direction, at_row, buffer in (
                (UP, place(UP, index) * chunk, 0), (DOWN, place(DOWN, index) * chunk, jnp.where(hop > 0, 1, 0)),
            )
            for owner in range(2)
        ])

        @pl.when(index == CHUNKS - 1)
        def _():
            def blocks(buffer, carry):
                make_blocks(jnp.where(buffer == 0, level(UP, hop), level(DOWN, hop)), buffer)
                return carry

            lax.fori_loop(0, jnp.where(hop > 0, 2, 1), blocks, 0)

        return carry

    lax.fori_loop(CHUNKS // 2, half * CHUNKS, step, 0)
    for number in range(full, rounds + 1):
        hear(number - 1)
        if number < rounds:
            tell(number)

    coef_ring(UP, half, level(UP, half)).wait_recv()
    where_block = lax.broadcasted_iota(jnp.int32, table.shape, 0)
    where_lane = lax.broadcasted_iota(jnp.int32, table.shape, 2)
    point = jnp.where(where_lane < local_k, where_block * local_k + where_lane, -1)
    coefs = table[...]
    for s in range(slots):
        chosen = jnp.sum(jnp.where(point == second[0, s], coefs, 0.0), axis=0)
        chosen = jnp.sum(chosen, axis=1, keepdims=True)
        picked[2 * s : 2 * s + 2, :] = jnp.broadcast_to(chosen[0:2, :], (2, picked.shape[1]))

    def send_end(direction):
        end_copy(direction, direction, core).start()

        @pl.when(jnp.logical_not(end_less) | (direction == DOWN))
        def _():
            end_copy(direction, direction, 1 - core).start()

        if direction == DOWN:

            @pl.when(end_more)
            def _():
                end_copy(UP, DOWN, 1 - core).start()

    def last_step(at, carry):
        @pl.when(at == 0)
        def _():
            for direction in (UP, DOWN):
                tail_copy(direction, 0, 1).wait_recv()
                tail_copy(direction, TAIL - 1, 0, shared, tail_send.at[1]).start()
                tail_pair(direction, 0).start()
            arrived(w_all.at[pl.ds(0, 2), :, pl.ds(0, short), :], pair_recv.at[full % 2])

        @pl.when((at > 0) & (at < TAIL - 1))
        def _():
            for direction in (UP, DOWN):
                tail_copy(direction, at, 1).wait_recv()
                pl.when(at == 1)(lambda direction=direction: send_end(direction))
                tail_pair(direction, at).start()
            arrived(w_all.at[pl.ds(0, 2), :, pl.ds(0, short), :], pair_recv.at[(full + at) % 2])

        @pl.when(at == TAIL - 1)
        def _():
            for direction in (UP, DOWN):
                tail_copy(direction, TAIL - 1, 1, shared).wait_recv()
                tail_pair(direction, TAIL - 1, shared, tail_pair_send.at[1]).start()
            arrived(w_all.at[pl.ds(0, 2), :, pl.ds(0, short), pl.ds(0, shared)], pair_recv.at[(full + TAIL - 1) % 2])
            arrived(w_all.at[pl.ds(0, 4), :, pl.ds(0, short), pl.ds(0, depth - shared)], end_recv)

        make_image(short, [
            (2 * level(UP, half) + owner, at_row, 0, owner * rows + at_row)
            for at_row in (tail_place(UP, at), tail_place(DOWN, at))
            for owner in range(2)
        ])
        return carry

    lax.fori_loop(0, TAIL, last_step, 0)
    make_blocks(level(UP, half), 0)

    totals = [jnp.zeros((bands, 2 * bands), jnp.float32) for _ in range(local_k)]
    for s in range(slots):
        block = acc[s, 0:bands, :] - turn(acc[s, bands:, :])
        term = block * picked[2 * s : 2 * s + 1, :] + turn(block) * picked[2 * s + 1 : 2 * s + 2, :]
        owner = first[0, s] - kb * local_k
        for k in range(local_k):
            totals[k] += jnp.where(owner == k, term, 0.0)
    take = bands // transfers
    for k in range(local_k):
        for to in range(transfers):
            stage[to, k * take : (k + 1) * take, :] = totals[k][to * take : (to + 1) * take, :]
    for i, (to, _) in enumerate(others):
        remote(stage.at[to], landed.at[i], sum_send, sum_recv, {"pb": to}).start()
    arrived(w_all.at[pl.ds(0, ring - 2)], ring_send)
    arrived(w_all.at[pl.ds(0, ring - 1)], pair_send)
    for sent in (tail_send, tail_pair_send):
        arrived(w_all.at[0, :, pl.ds(0, 2 * (TAIL - 1) * short), :], sent.at[0])
        arrived(w_all.at[0, :, pl.ds(0, 2 * short), pl.ds(0, shared)], sent.at[1])
    end_lanes = pl.ds(0, depth - shared)
    arrived(w_all.at[pl.ds(0, 2), :, pl.ds(0, short), end_lanes], end_send.at[DOWN])

    for sent, condition in (
        (1, end_less), (2, jnp.logical_not(end_less) & jnp.logical_not(end_more)), (3, end_more)
    ):

        @pl.when(condition)
        def _(sent=sent):
            arrived(w_all.at[pl.ds(0, sent), :, pl.ds(0, short), end_lanes], end_send.at[UP])

    arrived(table.at[pl.ds(0, 1 + 2 * (2 * half - 1))], coef_send)
    total = stage[pb]
    arrived(landed.at[pl.ds(0, transfers - 1)], sum_recv)
    for i in range(transfers - 1):
        total += landed[i]
    for k in range(local_k):
        for i in range(take // 2):
            even = total[k * take + 2 * i : k * take + 2 * i + 1, :]
            odd = total[k * take + 2 * i + 1 : k * take + 2 * i + 2, :]
            lanes = slice(i * 2 * bands, (i + 1) * 2 * bands)
            out_ref[k, 0:1, lanes] = jnp.where(lane < bands, even, pltpu.roll(odd, bands, axis=1))
            out_ref[k, 1:2, lanes] = jnp.where(lane < bands, pltpu.roll(even, bands, axis=1), odd)
    arrived(landed.at[pl.ds(0, transfers - 1)], sum_send)


def body(ring, transfers, screened, elem_val, elem_cond, pair_first, pair_second, coeffs):
    slots, _, _, bands, depth = elem_val.shape
    rows = screened.shape[2]
    local_k = coeffs.shape[0]
    half = ring // 2
    take = bands // transfers
    dma = pltpu.SemaphoreType.DMA
    width = slots * 2 * bands
    return pl.pallas_call(
        functools.partial(kernel, ring, transfers),
        out_shape=jax.ShapeDtypeStruct((local_k, 2, take * bands), jnp.float32),
        in_specs=[pl.BlockSpec(memory_space=pltpu.HBM)] * 6,
        out_specs=pl.BlockSpec(memory_space=pltpu.VMEM),
        scratch_shapes=[
            pltpu.VMEM((2 * ring, 2, rows, depth), jnp.bfloat16),
            pltpu.VMEM((width, depth), jnp.bfloat16),
            pltpu.VMEM((depth, width), jnp.bfloat16),
            pltpu.VMEM((slots, 2 * bands, depth), jnp.bfloat16),
            pltpu.VMEM((2, 2 * rows, width), jnp.bfloat16),
            pltpu.VMEM((slots, 2 * bands, 2 * bands), jnp.float32),
            pltpu.VMEM((2 * ring, 8, 128), jnp.float32),
            pltpu.VMEM((2 * slots, 128), jnp.float32),
            pltpu.VMEM((transfers, local_k * take, 2 * bands), jnp.float32),
            pltpu.VMEM((transfers, local_k * take, 2 * bands), jnp.float32),
            pltpu.SMEM((1, slots), jnp.int32),
            pltpu.SMEM((1, slots), jnp.int32),
            pltpu.VMEM((2, local_k), jnp.float32),
            dma((6,)),
            dma(()),
            dma((2, REUSE + TAIL)),
            dma(()),
            dma((2,)),
            dma(()),
            dma((2,)),
            dma((2,)),
            dma((2,)),
            dma(()),
            dma(()),
            dma((2, half)),
            dma(()),
            dma(()),
            dma(()),
            pltpu.SemaphoreType.REGULAR((2,)),
            pltpu.SemaphoreType.REGULAR((2,)),
        ],
        compiler_params=pltpu.CompilerParams(
            collective_id=0, has_side_effects=True, vmem_limit_bytes=40 * 1024 * 1024
        ),
        cost_estimate=pl.CostEstimate(
            flops=8 * depth * depth * slots * bands, bytes_accessed=8 * 1024 * 1024, transcendentals=0
        ),
    )(*(
        pltpu.with_memory_space_constraint(operand, pltpu.HBM)
        for operand in (
            screened, elem_val.reshape(width, depth), elem_cond.reshape(slots, 2 * bands, depth),
            pair_first.T, pair_second.T, coeffs.T,
        )
    ))


def solution(mesh):
    in_specs = (
        P("pb", None, "kb", None),
        P("kb", "pb", None, None, None),
        P("kb", "pb", None, None, None),
        P("kb", "pb"),
        P("kb", "pb"),
        P("kb", None),
    )
    out_specs = P("kb", None, "pb")
    ring, transfers = mesh.shape["kb"] // 2, mesh.shape["pb"]
    return jax.shard_map(
        functools.partial(body, ring, transfers), mesh=mesh, in_specs=in_specs, out_specs=out_specs, check_vma=False
    )
```

```python
import functools

import jax
import jax.numpy as jnp
from jax import lax
from jax.experimental import pallas as pl
from jax.experimental.pallas import tpu as pltpu
from jax.sharding import PartitionSpec as P

MESH = pl.DeviceIdType.MESH
CHUNKS = 4
FLIGHT = 2
TAIL = 4
REUSE = 6
DIRECT = 4
UP, DOWN = 0, 1


def side_of(transfers):
    return 1 << ((transfers.bit_length() - 1) // 2)


def rounds_of(ring, transfers):
    side = side_of(transfers)
    return 2 * (ring // 2) + side // 2 + transfers // side // 2 - 1


def kernel(
    ring, transfers, w_hbm, val_hbm, cond_hbm, first_hbm, second_hbm, coef_hbm, out_ref,
    w_all, val, val_t, cond, image, acc, table, picked, stage, landed, first, second, coef,
    local_sem, ring_send, ring_recv, pair_send, pair_recv, own_recv, tail_send, tail_pair_send, end_send, end_recv,
    coef_send, coef_recv, coef_pair_recv, sum_send, sum_recv, known, joined, met,
):
    half = ring // 2
    rows = w_hbm.shape[2]
    chunk = rows // CHUNKS
    slots = cond.shape[0]
    local_k = coef.shape[1]
    bands = cond.shape[1] // 2
    full = (half - 1) * CHUNKS
    short = rows // 2 // TAIL
    kb, pb = lax.axis_index("kb"), lax.axis_index("pb")
    z, core = kb // 2, kb % 2
    sibling = kb + 1 - 2 * core
    up = lax.rem(z + 1, ring) * 2 + core
    down = lax.rem(z + ring - 1, ring) * 2 + core

    side = side_of(transfers)
    y, x = pb // side, pb % side
    tall = transfers // side

    def hops(dy, dx):
        return min(dy, tall - dy) + min(dx, side - dx)

    others = sorted(
        ((dy, dx) for dy in range(tall) for dx in range(side) if dy or dx), key=lambda by: -hops(*by)
    )
    others = [(lax.rem(y + dy, tall) * side + lax.rem(x + dx, side), hops(dy, dx)) for dy, dx in others]
    plane = [other for other, far in others if far == 1]

    rounds = rounds_of(ring, transfers)

    def tell(number):
        for other in (up, down):
            pl.semaphore_signal(known.at[number % 2], inc=1, device_id={"kb": other}, device_id_type=MESH)

        @pl.when(z == 0)
        def _():
            for other in plane:
                pl.semaphore_signal(known.at[number % 2], inc=1, device_id={"pb": other}, device_id_type=MESH)

    def hear(number):
        pl.semaphore_wait(known.at[number % 2], jnp.where(z == 0, 2 + len(plane), 2))

    def level(direction, hop):
        return lax.rem(z + ring - hop, ring) if direction == UP else lax.rem(z + hop, ring)

    def place(direction, index):
        return index if direction == UP else CHUNKS - 1 - index

    def piece(block, index):
        return w_all.at[block, :, pl.ds(pl.multiple_of(index * chunk, chunk), chunk), :]

    def ring_copy(direction, number, src_hop):
        hop, index = number // CHUNKS + src_hop, place(direction, number % CHUNKS)
        block = 2 * level(direction, hop) + core
        return pltpu.make_async_remote_copy(
            src_ref=piece(block, index), dst_ref=piece(block, index),
            send_sem=ring_send, recv_sem=ring_recv.at[direction, number % REUSE],
            device_id={"kb": up if direction == UP else down}, device_id_type=MESH,
        )

    def first_copy(direction, number):
        index = place(direction, number)
        return pltpu.make_async_remote_copy(
            src_ref=w_hbm.at[0, :, pl.ds(index * chunk, chunk), :], dst_ref=piece(kb, index),
            send_sem=ring_send, recv_sem=ring_recv.at[direction, number % REUSE],
            device_id={"kb": up if direction == UP else down}, device_id_type=MESH,
        )

    def tail_place(direction, at):
        return pl.multiple_of(at * short if direction == UP else rows - (at + 1) * short, short)

    depth = w_hbm.shape[3]
    shared = depth - depth // DIRECT

    def tail_copy(direction, at, src_hop, lanes=depth, send_sem=tail_send.at[0]):
        block = 2 * level(direction, half - 1 + src_hop) + core
        part = w_all.at[block, :, pl.ds(tail_place(direction, at), short), pl.ds(0, lanes)]
        return remote(
            part, part, send_sem, ring_recv.at[direction, REUSE + at], {"kb": up if direction == UP else down}
        )

    def tail_pair(direction, at, lanes=depth, send_sem=tail_pair_send.at[0]):
        block = 2 * level(direction, half) + core
        part = w_all.at[block, :, pl.ds(tail_place(direction, at), short), pl.ds(0, lanes)]
        return remote(part, part, send_sem, pair_recv.at[(full + at) % 2], {"kb": sibling})

    def end_copy(direction, by, to_core):
        block = 2 * level(by, half - 1) + core
        part = w_all.at[block, :, pl.ds(tail_place(direction, TAIL - 1), short), pl.ds(shared, depth - shared)]
        chip = up - core if by == UP else down - core
        return remote(part, part, end_send.at[direction], end_recv, {"kb": chip + to_core})

    end_less, end_more = z == ring - 1, z == 1

    def pair(direction, number, owner):
        hop, index = number // CHUNKS + 1, place(direction, number % CHUNKS)
        block = 2 * level(direction, hop) + owner
        return pltpu.make_async_remote_copy(
            src_ref=piece(block, index), dst_ref=piece(block, index),
            send_sem=pair_send, recv_sem=pair_recv.at[number % 2],
            device_id={"kb": sibling}, device_id_type=MESH,
        )

    def remote(src, dst, send_sem, recv_sem, device):
        return pltpu.make_async_remote_copy(
            src_ref=src, dst_ref=dst, send_sem=send_sem, recv_sem=recv_sem, device_id=device, device_id_type=MESH
        )

    def arrived(ref, sem):
        pltpu.make_async_copy(ref, ref, sem).wait()

    def own_pair(owner):
        return remote(w_hbm.at[0], w_all.at[owner], pair_send, own_recv, {"kb": sibling})

    def coef_pair(owner):
        return remote(table.at[owner], table.at[owner], coef_send, coef_pair_recv, {"kb": sibling})

    def coef_ring(direction, hop, at):
        both = table.at[pl.ds(2 * at, 2)]
        return remote(
            both, both, coef_send, coef_recv.at[direction, hop - 1], {"kb": up if direction == UP else down}
        )

    lane = lax.broadcasted_iota(jnp.int32, (1, 2 * bands), 1)
    minus_plus = jnp.where(lane < bands, -1.0, 1.0)

    def turn(block):
        return pltpu.roll(block, bands, axis=1) * minus_plus

    def make_image(size, pieces):
        rows_in = jnp.concatenate(
            [
                w_all[block, part, pl.ds(pl.multiple_of(first_row, size), size), :]
                for block, first_row, _, _ in pieces
                for part in range(2)
            ],
            axis=0,
        )
        for pair_of in range(slots // 2):
            wide = slice(pair_of * 4 * bands, (pair_of + 1) * 4 * bands)
            product = jnp.dot(rows_in, val_t[:, wide], preferred_element_type=jnp.float32)
            for i, (_, _, buffer, row) in enumerate(pieces):
                by_real = product[2 * i * size : (2 * i + 1) * size]
                by_imag = product[(2 * i + 1) * size : (2 * i + 2) * size]
                for s in range(2):
                    lanes = slice(s * 2 * bands, (s + 1) * 2 * bands)
                    to = (pair_of * 2 + s) * 2 * bands
                    image[buffer, pl.ds(pl.multiple_of(row, size), size), to : to + 2 * bands] = (
                        by_real[:, lanes] + turn(by_imag[:, lanes])
                    ).astype(jnp.bfloat16)

    def make_blocks(at, buffer):
        columns = pl.ds(pl.multiple_of(at * 2 * rows, 2 * rows), 2 * rows)
        for s in range(slots):
            acc[s] += jnp.dot(
                cond[s, :, columns],
                image[buffer, :, s * 2 * bands : (s + 1) * 2 * bands],
                preferred_element_type=jnp.float32,
            )

    loads = [
        pltpu.make_async_copy(src, dst, local_sem.at[i])
        for i, (src, dst) in enumerate((
            (coef_hbm, coef), (val_hbm, val), (w_hbm.at[0], w_all.at[kb]), (cond_hbm, cond),
            (first_hbm, first), (second_hbm, second),
        ))
    ]
    barrier = pltpu.get_barrier_semaphore()

    def first_out(direction):
        for number in range(FLIGHT):
            first_copy(direction, number).start()

    above_is_nearer, below_is_nearer = z >= half, (z > 0) & (z <= half)

    @pl.when(jnp.logical_not(above_is_nearer))
    def _():
        pl.semaphore_signal(barrier, inc=1, device_id={"kb": up}, device_id_type=MESH)

    @pl.when(jnp.logical_not(below_is_nearer))
    def _():
        pl.semaphore_signal(barrier, inc=1, device_id={"kb": down}, device_id_type=MESH)

    @pl.when(core == 1)
    def _():
        pl.semaphore_signal(barrier, inc=1, device_id={"kb": sibling}, device_id_type=MESH)

    @pl.when(z == 0)
    def _():
        for other in plane:
            pl.semaphore_signal(barrier, inc=1, device_id={"pb": other}, device_id_type=MESH)

    pl.semaphore_wait(barrier, jnp.where(z == 0, len(plane), jnp.where(z == half, 2, 1)) + 1 - core)

    @pl.when(above_is_nearer)
    def _():
        pl.semaphore_signal(joined.at[DOWN], inc=1, device_id={"kb": up}, device_id_type=MESH)
        first_out(UP)

    @pl.when(below_is_nearer)
    def _():
        pl.semaphore_signal(joined.at[UP], inc=1, device_id={"kb": down}, device_id_type=MESH)
        first_out(DOWN)

    @pl.when(core == 0)
    def _():
        pl.semaphore_signal(met, inc=1, device_id={"kb": sibling}, device_id_type=MESH)

    for load in loads:
        load.start()

    @pl.when(jnp.logical_not(above_is_nearer))
    def _():
        pl.semaphore_wait(joined.at[UP], 1)
        first_out(UP)

    @pl.when(jnp.logical_not(below_is_nearer))
    def _():
        pl.semaphore_wait(joined.at[DOWN], 1)
        first_out(DOWN)

    @pl.when(core == 1)
    def _():
        pl.semaphore_wait(met, 1)

    own_pair(kb).start()

    table[kb] = jnp.zeros_like(table[0])
    loads[0].wait()
    table[kb, 0:2, 0:local_k] = coef[...]
    coef_pair(kb).start()
    acc[...] = jnp.zeros_like(acc)
    loads[1].wait()

    def transpose(k, carry):
        columns = pl.ds(pl.multiple_of(k * 256, 256), 256)
        val_t[columns, :] = val[:, columns].T
        return carry

    lax.fori_loop(0, val.shape[1] // 256, transpose, 0)
    coef_pair(sibling).wait_recv()
    coef_ring(UP, 1, z).start()
    coef_ring(DOWN, 1, z).start()
    for load in loads[2:]:
        load.wait()
    own_pair(sibling).wait_recv()

    def step(at, carry):
        hop, index = at // CHUNKS, at % CHUNKS
        number = at - CHUNKS
        later = number + FLIGHT

        @pl.when(hop > 0)
        def _():
            for direction in (UP, DOWN):
                ring_copy(direction, number, 1).wait_recv()

                @pl.when(later < full)
                def _():
                    ring_copy(direction, later, 0).start()

                @pl.when(later == full)
                def _():
                    tail_copy(direction, 0, 0).start()

                @pl.when(later == full + 1)
                def _():
                    for at in range(1, TAIL - 1):
                        tail_copy(direction, at, 0).start()

                pair(direction, number, core).start()

        @pl.when((number > 0) & (number <= rounds))
        def _():
            hear(number - 1)

        @pl.when((number >= 0) & (number < rounds))
        def _():
            tell(number)

        @pl.when((hop > 0) & (index == 0))
        def _():
            coef_ring(UP, hop, level(UP, hop)).wait_recv()
            coef_ring(UP, hop + 1, level(UP, hop)).start()
            coef_ring(DOWN, hop, level(DOWN, hop)).wait_recv()

            @pl.when(hop < half - 1)
            def _():
                coef_ring(DOWN, hop + 1, level(DOWN, hop)).start()

        @pl.when(hop > 0)
        def _():
            arrived(w_all.at[pl.ds(0, 2), :, pl.ds(0, chunk), :], pair_recv.at[number % 2])

        make_image(chunk, [
            (2 * level(direction, hop) + owner, at_row, buffer, owner * rows + at_row)
            for direction, at_row, buffer in (
                (UP, place(UP, index) * chunk, 0), (DOWN, place(DOWN, index) * chunk, jnp.where(hop > 0, 1, 0)),
            )
            for owner in range(2)
        ])

        @pl.when(index == CHUNKS - 1)
        def _():
            def blocks(buffer, carry):
                make_blocks(jnp.where(buffer == 0, level(UP, hop), level(DOWN, hop)), buffer)
                return carry

            lax.fori_loop(0, jnp.where(hop > 0, 2, 1), blocks, 0)

        return carry

    lax.fori_loop(CHUNKS // 2, half * CHUNKS, step, 0)
    for number in range(full, rounds + 1):
        hear(number - 1)
        if number < rounds:
            tell(number)

    coef_ring(UP, half, level(UP, half)).wait_recv()
    where_block = lax.broadcasted_iota(jnp.int32, table.shape, 0)
    where_lane = lax.broadcasted_iota(jnp.int32, table.shape, 2)
    point = jnp.where(where_lane < local_k, where_block * local_k + where_lane, -1)
    coefs = table[...]
    for s in range(slots):
        chosen = jnp.sum(jnp.where(point == second[0, s], coefs, 0.0), axis=0)
        chosen = jnp.sum(chosen, axis=1, keepdims=True)
        picked[2 * s : 2 * s + 2, :] = jnp.broadcast_to(chosen[0:2, :], (2, picked.shape[1]))

    def send_end(direction):
        end_copy(direction, direction, core).start()

        @pl.when(jnp.logical_not(end_less) | (direction == DOWN))
        def _():
            end_copy(direction, direction, 1 - core).start()

        if direction == DOWN:

            @pl.when(end_more)
            def _():
                end_copy(UP, DOWN, 1 - core).start()

    def last_step(at, carry):
        @pl.when(at == 0)
        def _():
            for direction in (UP, DOWN):
                tail_copy(direction, 0, 1).wait_recv()
                tail_copy(direction, TAIL - 1, 0, shared, tail_send.at[1]).start()
                tail_pair(direction, 0).start()
            arrived(w_all.at[pl.ds(0, 2), :, pl.ds(0, short), :], pair_recv.at[full % 2])

        @pl.when((at > 0) & (at < TAIL - 1))
        def _():
            for direction in (UP, DOWN):
                tail_copy(direction, at, 1).wait_recv()
                pl.when(at == 1)(lambda direction=direction: send_end(direction))
                tail_pair(direction, at).start()
            arrived(w_all.at[pl.ds(0, 2), :, pl.ds(0, short), :], pair_recv.at[(full + at) % 2])

        @pl.when(at == TAIL - 1)
        def _():
            for direction in (UP, DOWN):
                tail_copy(direction, TAIL - 1, 1, shared).wait_recv()
                tail_pair(direction, TAIL - 1, shared, tail_pair_send.at[1]).start()
            arrived(w_all.at[pl.ds(0, 2), :, pl.ds(0, short), pl.ds(0, shared)], pair_recv.at[(full + TAIL - 1) % 2])
            arrived(w_all.at[pl.ds(0, 4), :, pl.ds(0, short), pl.ds(0, depth - shared)], end_recv)

        make_image(short, [
            (2 * level(UP, half) + owner, at_row, 0, owner * rows + at_row)
            for at_row in (tail_place(UP, at), tail_place(DOWN, at))
            for owner in range(2)
        ])
        return carry

    lax.fori_loop(0, TAIL, last_step, 0)
    make_blocks(level(UP, half), 0)

    totals = [jnp.zeros((bands, 2 * bands), jnp.float32) for _ in range(local_k)]
    for s in range(slots):
        block = acc[s, 0:bands, :] - turn(acc[s, bands:, :])
        term = block * picked[2 * s : 2 * s + 1, :] + turn(block) * picked[2 * s + 1 : 2 * s + 2, :]
        owner = first[0, s] - kb * local_k
        for k in range(local_k):
            totals[k] += jnp.where(owner == k, term, 0.0)
    take = bands // transfers
    for k in range(local_k):
        for to in range(transfers):
            stage[to, k * take : (k + 1) * take, :] = totals[k][to * take : (to + 1) * take, :]
    for i, (to, _) in enumerate(others):
        remote(stage.at[to], landed.at[i], sum_send, sum_recv, {"pb": to}).start()
    arrived(w_all.at[pl.ds(0, ring - 2)], ring_send)
    arrived(w_all.at[pl.ds(0, ring - 1)], pair_send)
    for sent in (tail_send, tail_pair_send):
        arrived(w_all.at[0, :, pl.ds(0, 2 * (TAIL - 1) * short), :], sent.at[0])
        arrived(w_all.at[0, :, pl.ds(0, 2 * short), pl.ds(0, shared)], sent.at[1])
    end_lanes = pl.ds(0, depth - shared)
    arrived(w_all.at[pl.ds(0, 2), :, pl.ds(0, short), end_lanes], end_send.at[DOWN])

    for sent, condition in (
        (1, end_less), (2, jnp.logical_not(end_less) & jnp.logical_not(end_more)), (3, end_more)
    ):

        @pl.when(condition)
        def _(sent=sent):
            arrived(w_all.at[pl.ds(0, sent), :, pl.ds(0, short), end_lanes], end_send.at[UP])

    arrived(table.at[pl.ds(0, 1 + 2 * (2 * half - 1))], coef_send)
    total = stage[pb]
    arrived(landed.at[pl.ds(0, transfers - 1)], sum_recv)
    for i in range(transfers - 1):
        total += landed[i]
    for k in range(local_k):
        for i in range(take // 2):
            even = total[k * take + 2 * i : k * take + 2 * i + 1, :]
            odd = total[k * take + 2 * i + 1 : k * take + 2 * i + 2, :]
            lanes = slice(i * 2 * bands, (i + 1) * 2 * bands)
            out_ref[k, 0:1, lanes] = jnp.where(lane < bands, even, pltpu.roll(odd, bands, axis=1))
            out_ref[k, 1:2, lanes] = jnp.where(lane < bands, pltpu.roll(even, bands, axis=1), odd)
    arrived(landed.at[pl.ds(0, transfers - 1)], sum_send)


def body(ring, transfers, screened, elem_val, elem_cond, pair_first, pair_second, coeffs):
    slots, _, _, bands, depth = elem_val.shape
    rows = screened.shape[2]
    local_k = coeffs.shape[0]
    half = ring // 2
    take = bands // transfers
    dma = pltpu.SemaphoreType.DMA
    width = slots * 2 * bands
    return pl.pallas_call(
        functools.partial(kernel, ring, transfers),
        out_shape=jax.ShapeDtypeStruct((local_k, 2, take * bands), jnp.float32),
        in_specs=[pl.BlockSpec(memory_space=pltpu.HBM)] * 6,
        out_specs=pl.BlockSpec(memory_space=pltpu.VMEM),
        scratch_shapes=[
            pltpu.VMEM((2 * ring, 2, rows, depth), jnp.bfloat16),
            pltpu.VMEM((width, depth), jnp.bfloat16),
            pltpu.VMEM((depth, width), jnp.bfloat16),
            pltpu.VMEM((slots, 2 * bands, depth), jnp.bfloat16),
            pltpu.VMEM((2, 2 * rows, width), jnp.bfloat16),
            pltpu.VMEM((slots, 2 * bands, 2 * bands), jnp.float32),
            pltpu.VMEM((2 * ring, 8, 128), jnp.float32),
            pltpu.VMEM((2 * slots, 128), jnp.float32),
            pltpu.VMEM((transfers, local_k * take, 2 * bands), jnp.float32),
            pltpu.VMEM((transfers, local_k * take, 2 * bands), jnp.float32),
            pltpu.SMEM((1, slots), jnp.int32),
            pltpu.SMEM((1, slots), jnp.int32),
            pltpu.VMEM((2, local_k), jnp.float32),
            dma((6,)),
            dma(()),
            dma((2, REUSE + TAIL)),
            dma(()),
            dma((2,)),
            dma(()),
            dma((2,)),
            dma((2,)),
            dma((2,)),
            dma(()),
            dma(()),
            dma((2, half)),
            dma(()),
            dma(()),
            dma(()),
            pltpu.SemaphoreType.REGULAR((2,)),
            pltpu.SemaphoreType.REGULAR((2,)),
            pltpu.SemaphoreType.REGULAR,
        ],
        compiler_params=pltpu.CompilerParams(
            collective_id=0, has_side_effects=True, vmem_limit_bytes=40 * 1024 * 1024
        ),
        cost_estimate=pl.CostEstimate(
            flops=8 * depth * depth * slots * bands, bytes_accessed=8 * 1024 * 1024, transcendentals=0
        ),
    )(*(
        pltpu.with_memory_space_constraint(operand, pltpu.HBM)
        for operand in (
            screened, elem_val.reshape(width, depth), elem_cond.reshape(slots, 2 * bands, depth),
            pair_first.T, pair_second.T, coeffs.T,
        )
    ))


def solution(mesh):
    in_specs = (
        P("pb", None, "kb", None),
        P("kb", "pb", None, None, None),
        P("kb", "pb", None, None, None),
        P("kb", "pb"),
        P("kb", "pb"),
        P("kb", None),
    )
    out_specs = P("kb", None, "pb")
    ring, transfers = mesh.shape["kb"] // 2, mesh.shape["pb"]
    return jax.shard_map(
        functools.partial(body, ring, transfers), mesh=mesh, in_specs=in_specs, out_specs=out_specs, check_vma=False
    )
```
